32 devices in a mesh: days: 2 (over y), chan: 4 (over z), tm: 2 (over x), freq: 2 (over core).
Axes of the slice: x: 2, y: 2, z: 4, core: 2. Of those that a mesh axis runs over, the one named last changes fastest.
Arguments:
- recording: bfloat16 [2048, 2048], P(('days', 'chan', 'freq'), 'tm'), parts along dimension 0, may hold values from -6 to 6
- trailing: bfloat16 [2048, 1024], P(('days', 'chan', 'freq')), parts along dimension 0, may hold values from -6 to 6
- whiten_filter: bfloat16 [1024, 64], P(('chan', 'freq')), may hold values from -0.75 to 0.75
- pair_list: int32 [8, 4], P(('days', 'chan')), parts along dimension 0, may hold values from -1 to 3, as said below
Outputs:
- cross_spectra: float32 [8, 4, 4, 2, 256, 256], P(('days', 'chan'), None, ('tm', 'freq')), parts along dimension 0
The draws below stay inside these ranges and needn't reach their ends.
There are 2 independent parts, one for each index of `days`. The reference program is written for one: setup_inputs(seed, part) draws one part's arguments, and reference() takes and returns one part's arrays. A program takes and returns all parts, laid end to end along the dimension named above; an argument that names none is the same for every part. Nothing has to cross between parts.
Inputs may be any that keep to these rules, and one draw needn't show every extreme that they name: `pair_list`: row a lists in its first slots distinct blocks b with |b - a| <= 3, then -1 in the remaining slots; every row lists at least one block, and some row of every draw fills all 4 slots.
All inputs are finite; a program needn't handle non-finite values.
Results may differ from the reference program's by a relative error of at most 0.0046.
Values may be sent and summed in bfloat16 or wider, within the bound.
No kernel may reach another device: no remote copies, remote signals or barrier semaphores. Data moves between devices by JAX's collectives and lax.ppermute only.
A program may use at most 64 MiB of HBM per device.

```python
import math
import jax
import jax.numpy as jnp
from jax import lax

BLK = 256
WHIT = 64
WIN = 2048
FB = 512
REACH = 3
SLOTS = 4
HOP = 1024
NB = 4
CHANNELS = 1024
SEGS = 2
SAMPLES = 2048
BANDS = 4
BANDW = 128
N_CHAN = 4


def draw_pair_list(key, part):
    first_key = jax.random.fold_in(key, 11)
    second_key = jax.random.fold_in(key, 12)
    third_key = jax.random.fold_in(key, 13)
    fourth_key = jax.random.fold_in(key, 14)
    spread = 2 * REACH + 1
    owners = jnp.arange(NB, dtype=jnp.int32)[:, None]
    columns = jnp.arange(spread, dtype=jnp.int32)[None, :]
    candidates = owners + columns - REACH
    is_valid = (candidates >= 0) & (candidates < NB)
    scores = jax.random.randint(first_key, (NB, spread), 0, 65536, dtype=jnp.int32) * spread + columns
    scores = jnp.where(is_valid, scores, -1)
    ranking = jnp.argsort(-scores, axis=1, stable=True)
    picked = jnp.take_along_axis(candidates, ranking, axis=1)[:, :SLOTS]
    counts = jax.random.randint(second_key, (NB,), 1, 3, dtype=jnp.int32)
    is_heavy = jax.random.randint(third_key, (NB,), 0, 4, dtype=jnp.int32) == 0
    counts = jnp.where(is_heavy, SLOTS, counts)
    forced = jax.random.randint(fourth_key, (), 0, NB, dtype=jnp.int32)
    counts = jnp.where(jnp.arange(NB, dtype=jnp.int32) == forced, SLOTS, counts)
    counts = jnp.minimum(counts, SLOTS)
    slot_index = jnp.arange(SLOTS, dtype=jnp.int32)[None, :]
    return jnp.where(slot_index < counts[:, None], picked, -1).astype(jnp.int32)


def shard_levels(rng, extent, split, least, top_value):
    def one(dim, shards_of):
        steps = jax.random.uniform(jax.random.fold_in(jax.random.fold_in(rng, 6), dim), (shards_of,), jnp.float32, least / len(split), top_value / len(split))
        return jnp.repeat(jnp.exp(steps), extent[dim] // shards_of).reshape((-1,) + (1,) * (len(extent) - dim - 1))

    loudness = one(*split[0])
    for cut in split[1:]:
        loudness = loudness * one(*cut)
    return loudness


def bell_draw(rng, extent, scale, bound, cuts=(), kind=jnp.bfloat16):
    array = scale * jax.random.normal(rng, extent, jnp.float32)
    if cuts:
        array = array * shard_levels(rng, extent, cuts, -0.22, 0.18)
    return jnp.clip(array, -bound, bound).astype(kind)


def setup_inputs(seed: int = 0, part: int = 0) -> dict:
    seeds = jax.random.split(jax.random.key(seed), 5)
    part_keys = jax.random.split(jax.random.fold_in(seeds[4], part), 5)
    recording = bell_draw(part_keys[0], (CHANNELS, SAMPLES), 1.0, 6.0, ((0, 8), (1, 2)))
    trailing = bell_draw(part_keys[1], (CHANNELS, HOP), 1.0, 6.0, ((0, 8),))
    whiten_filter = bell_draw(seeds[2], (CHANNELS, WHIT), WHIT ** -0.5, 0.75, ((0, 8),))
    pair_list = draw_pair_list(jax.random.fold_in(jax.random.fold_in(seeds[4], part), 71), part)
    return dict(recording=recording, trailing=trailing, whiten_filter=whiten_filter, pair_list=pair_list)


def fourier_table(first_bin, bin_count, length):
    samples = jnp.arange(length, dtype=jnp.int32)[:, None]
    bin_index = first_bin + jnp.arange(bin_count, dtype=jnp.int32)[None, :]
    phase = samples * bin_index % length
    angle = 2.0 * math.pi / length * phase.astype(jnp.float32)
    taper = 0.5 - 0.5 * jnp.cos(2.0 * math.pi / length * jnp.arange(length, dtype=jnp.int32).astype(jnp.float32))
    normaliser = 1.0 / math.sqrt(0.375 * length)
    cosine = (taper[:, None] * jnp.cos(angle) * normaliser).astype(jnp.bfloat16)
    sine_table = (-taper[:, None] * jnp.sin(angle) * normaliser).astype(jnp.bfloat16)
    return (cosine, sine_table)

def reference(recording, trailing, whiten_filter, pair_list):
    signal = jnp.concatenate([recording, trailing], axis=1)
    channels = signal.shape[0]
    cosine, sine_table = fourier_table(0, FB, WIN)
    joined = jnp.concatenate([cosine, sine_table], axis=1).astype(jnp.float32)

    def transform(segment):
        start = (segment * HOP).astype(jnp.int32)
        pieces = lax.dynamic_slice_in_dim(signal, start, WIN, 1)
        return jnp.dot(pieces.astype(jnp.float32), joined).astype(jnp.bfloat16)
    raw = lax.map(transform, jnp.arange(SEGS, dtype=jnp.int32))
    raw = raw.transpose(1, 0, 2).reshape(channels, SEGS * 2 * FB)
    rim_width = WHIT // 2
    padded = jnp.pad(raw, ((rim_width, rim_width), (0, 0)))
    offset = jnp.arange(BLK + WHIT, dtype=jnp.int32)[None, :] - jnp.arange(BLK, dtype=jnp.int32)[:, None]
    inside = (offset >= 0) & (offset < WHIT)
    clipped = jnp.clip(offset, 0, WHIT - 1)

    def whiten_block(index):
        start = (index * BLK).astype(jnp.int32)
        window_rows = lax.dynamic_slice_in_dim(padded, start, BLK + WHIT, 0)
        weight_rows = lax.dynamic_slice_in_dim(whiten_filter, start, BLK, 0)
        band_matrix = jnp.where(inside, jnp.take_along_axis(weight_rows, clipped, axis=1), jnp.zeros((), weight_rows.dtype))
        predicted = jnp.dot(band_matrix.astype(jnp.float32), window_rows.astype(jnp.float32))
        own_rows = lax.dynamic_slice_in_dim(raw, start, BLK, 0)
        return (own_rows.astype(jnp.float32) - predicted).astype(jnp.bfloat16)
    spectra = lax.map(whiten_block, jnp.arange(N_CHAN, dtype=jnp.int32))
    arranged = spectra.reshape(NB, BLK, SEGS, 2, BANDS, BANDW).transpose(0, 3, 4, 1, 2, 5)
    arranged = arranged.reshape(NB, 2, BANDS, BLK, SEGS * BANDW)
    scaling = 1.0 / math.sqrt(SEGS * BANDW)

    def owner(owner_index):
        own_block = lax.dynamic_index_in_dim(arranged, owner_index, 0, keepdims=False).astype(jnp.float32)

        def one_slot(partner_index):
            partner = lax.dynamic_index_in_dim(arranged, jnp.maximum(partner_index, 0), 0, keepdims=False).astype(jnp.float32)
            real_part = jnp.einsum('gik,gjk->gij', own_block[0], partner[0]) + jnp.einsum('gik,gjk->gij', own_block[1], partner[1])
            imag_part = jnp.einsum('gik,gjk->gij', own_block[1], partner[0]) - jnp.einsum('gik,gjk->gij', own_block[0], partner[1])
            crossed = jnp.stack([real_part, imag_part], axis=1) * scaling
            return jnp.where(partner_index >= 0, crossed, jnp.zeros((), crossed.dtype))
        return lax.map(one_slot, lax.dynamic_index_in_dim(pair_list, owner_index, 0, keepdims=False))
    return lax.map(owner, jnp.arange(NB, dtype=jnp.int32))
```

```python
import functools
import math

import jax
import jax.numpy as jnp
import ml_dtypes
import numpy as np
from jax import lax
from jax.experimental import pallas as pl
from jax.experimental.pallas import tpu as pltpu
from jax.sharding import PartitionSpec as P

FB = 512
REACH = 3
SLOTS = 4
LANES = 128


def band_tables(bands, length):
    samples = np.arange(length, dtype=np.int64)[:, None]
    bins = np.arange(FB, dtype=np.int64)[None, :]
    phase = (samples * bins % length).astype(np.float32)
    angle = np.float32(2.0 * math.pi / length) * phase
    ramp = np.float32(2.0 * math.pi / length) * np.arange(length, dtype=np.float32)
    taper = (np.float32(0.5) - np.float32(0.5) * np.cos(ramp))[:, None]
    normaliser = np.float32(1.0 / math.sqrt(0.375 * length))
    cosine = (taper * np.cos(angle) * normaliser).astype(ml_dtypes.bfloat16)
    sine = (-taper * np.sin(angle) * normaliser).astype(ml_dtypes.bfloat16)
    both = np.stack([cosine, sine], axis=1).reshape(length, 2, bands, FB // bands)
    return np.ascontiguousarray(both.transpose(2, 0, 1, 3)).reshape(bands, length, 2 * FB // bands)


def swapped(value, axis):
    return lax.ppermute(value, axis, [(0, 1), (1, 0)])


def transform_kernel(span_count, *refs):
    own, other = refs[: span_count + 1], refs[span_count + 1 : 2 * span_count + 2]
    table, out, signal = refs[2 * span_count + 2 :]
    span, half = lax.axis_index("tm"), lax.axis_index("freq")
    rows, hop = own[0].shape
    for group, which in ((own, half), (other, 1 - half)):
        base = pl.multiple_of(which * rows, rows)
        for step in range(span_count):
            place = lax.rem(span - step + span_count, span_count)
            signal[pl.ds(base, rows), pl.ds(pl.multiple_of(place * hop, hop), hop)] = group[step][...]
        signal[pl.ds(base, rows), span_count * hop :] = group[span_count][...]
    for segment in range(span_count):
        window = signal[:, segment * hop : (segment + 2) * hop]
        product = jnp.dot(window, table[...], preferred_element_type=jnp.float32)
        out[segment] = product.astype(jnp.bfloat16)


def band_kernel(weights, out):
    blocks, rows, width = out.shape
    taps = weights.shape[1]
    for block in range(blocks):
        tile = weights[block * rows : (block + 1) * rows, :].astype(jnp.float32)
        wide = jnp.concatenate([tile, jnp.zeros((rows, width - taps), jnp.float32)], axis=1)
        out[block] = pltpu.roll(wide, 0, 1, stride=1, stride_axis=0).astype(jnp.bfloat16)


def cross_kernel(places, rims, scaling, slots, where, *refs):
    count = len(places)
    blocks, refs = refs[:count], refs[count:]
    edges, refs = refs[:rims], refs[rims:]
    band, out, padded, own_left, own_flip = refs
    segments, rows, width = blocks[0].shape
    total = padded.shape[1]
    rim = 32
    slot = pl.program_id(0)

    def whitened(block):
        start = pl.multiple_of(block * rows, rows)
        matrix = band[block]
        result = []
        for segment in range(segments):
            window = padded[segment, pl.ds(start, matrix.shape[1]), :]
            predicted = jnp.dot(matrix, window, preferred_element_type=jnp.float32)
            raw = padded[segment, pl.ds(pl.multiple_of(start + rim, rim), rows), :]
            result.append((raw.astype(jnp.float32) - predicted).astype(jnp.bfloat16))
        return result

    @pl.when(slot == 0)
    def _():
        first = jnp.zeros((segments, rim, width), jnp.bfloat16)
        padded[:, :rim, :] = edges[0][...] if rims else first
        if rims:
            padded[:, total - 3 * rim : total - 2 * rim, :] = edges[1][...]
        else:
            padded[:, total - 3 * rim : total - 2 * rim, :] = first
        padded[:, total - 2 * rim :, :] = jnp.zeros((segments, 2 * rim, width), jnp.bfloat16)
        for index in range(count):
            start = pl.multiple_of(where[index] * rows + rim, rim)
            padded[:, pl.ds(start, rows), :] = blocks[index][...]
        mine = whitened(where[0])
        half = width // 2
        for segment in range(segments):
            own_left[segment] = mine[segment]
            own_flip[segment] = jnp.concatenate(
                [mine[segment][:, half:], -mine[segment][:, :half]], axis=1
            )

    partner = slots[slot]

    @pl.when(partner >= 0)
    def _():
        theirs = whitened(partner)
        contract = (((1,), (1,)), ((), ()))
        for part, left in enumerate((own_left, own_flip)):
            value = jnp.zeros((rows, rows), jnp.float32)
            for segment in range(segments):
                value += lax.dot_general(
                    left[segment], theirs[segment], contract, preferred_element_type=jnp.float32
                )
            out[0, part] = value * scaling

    @pl.when(partner < 0)
    def _():
        out[...] = jnp.zeros(out.shape, out.dtype)


def local(tables, recording, trailing, whiten_filter, pair_list):
    rows, hop = recording.shape
    spans, halves, chain = (lax.axis_size(axis) for axis in ("tm", "freq", "chan"))
    bands = spans * halves
    bins2 = 2 * FB // bands
    block_rows = halves * rows
    taps = whiten_filter.shape[1]
    rim = taps // 2
    here = lax.axis_index("chan")

    own = [recording]
    for step in range(1, spans):
        own.append(lax.ppermute(recording, "tm", [(i, (i + step) % spans) for i in range(spans)]))
    own.append(trailing)
    other = [swapped(value, "freq") for value in own]
    band_index = lax.axis_index("tm") * halves + lax.axis_index("freq")
    table = lax.dynamic_index_in_dim(tables, band_index, 0, keepdims=False)
    raw = pl.pallas_call(
        functools.partial(transform_kernel, spans),
        out_shape=jax.ShapeDtypeStruct((spans, block_rows, bins2), jnp.bfloat16),
        scratch_shapes=[pltpu.VMEM((block_rows, (spans + 1) * hop), jnp.bfloat16)],
        compiler_params=pltpu.CompilerParams(vmem_limit_bytes=24 * 2**20),
        name="transform",
    )(*own, *other, table)

    everyone = lax.all_gather(whiten_filter, ("chan", "freq"), axis=0, tiled=True)
    if chain == 4:
        send = lambda value, route: lax.ppermute(value, "chan", route)
        first = send(raw, [(0, 2), (2, 3), (3, 1), (1, 0)])
        second = send(raw, [(1, 3), (3, 2), (2, 0), (0, 1)])
        third = send(raw, [(1, 2), (2, 1)])
        fourth = send(first, [(2, 3), (1, 0)])
        inner = (here == 1) | (here == 2)
        blocks = [raw, first, second, jnp.where(inner, third, fourth)]
        pick = lambda *options: jnp.array(options, jnp.int32)[here]
        places = [here, pick(1, 3, 0, 2), pick(2, 0, 3, 1), pick(3, 2, 1, 0)]
        edges, near = [], chain
        base = jnp.int32(0)
        weights = everyone
    else:
        def shifted(value, distance):
            route = [(i - distance, i) for i in range(chain) if 0 <= i - distance < chain]
            return lax.ppermute(value, "chan", route)

        blocks, places = [raw], [jnp.int32(REACH)]
        for distance in range(-REACH, REACH + 1):
            if distance:
                blocks.append(shifted(raw, -distance))
                places.append(jnp.int32(distance + REACH))
        edges = [
            shifted(raw[:, block_rows - rim :, :], REACH + 1),
            shifted(raw[:, :rim, :], -REACH - 1),
        ]
        near = 2 * REACH + 1
        base = here - REACH
        beyond = jnp.pad(everyone, ((REACH * block_rows, REACH * block_rows), (0, 0)))
        weights = lax.dynamic_slice_in_dim(beyond, here * block_rows, near * block_rows, 0)
    window = -(-(block_rows + taps) // LANES) * LANES
    band = pl.pallas_call(
        band_kernel,
        out_shape=jax.ShapeDtypeStruct((near, block_rows, window), jnp.bfloat16),
        compiler_params=pltpu.CompilerParams(vmem_limit_bytes=24 * 2**20),
        name="band_matrix",
    )(weights)

    slots = pair_list[0]
    slots = jnp.where(slots >= 0, slots - base, -1)
    where = jnp.stack(places).astype(jnp.int32)
    whole = lambda shape: pl.BlockSpec(shape, lambda i, *_: (0,) * len(shape))
    result = pl.pallas_call(
        functools.partial(
            cross_kernel, places, len(edges), 1.0 / math.sqrt(spans * bins2 // 2)
        ),
        out_shape=jax.ShapeDtypeStruct((SLOTS, 2, block_rows, block_rows), jnp.float32),
        grid_spec=pltpu.PrefetchScalarGridSpec(
            num_scalar_prefetch=2,
            grid=(SLOTS,),
            in_specs=[whole(value.shape) for value in (*blocks, *edges, band)],
            out_specs=pl.BlockSpec((1, 2, block_rows, block_rows), lambda i, *_: (i, 0, 0, 0)),
            scratch_shapes=[
                pltpu.VMEM((spans, near * block_rows + 4 * rim, bins2), jnp.bfloat16),
                pltpu.VMEM((spans, block_rows, bins2), jnp.bfloat16),
                pltpu.VMEM((spans, block_rows, bins2), jnp.bfloat16),
            ],
        ),
        compiler_params=pltpu.CompilerParams(vmem_limit_bytes=32 * 2**20),
        name="cross",
    )(slots, where, *blocks, *edges, band)
    return result.reshape(1, SLOTS, 1, 2, block_rows, block_rows)


def solution(mesh):
    placed = (
        P(("days", "chan", "freq"), "tm"),
        P(("days", "chan", "freq"), None),
        P(("chan", "freq"), None),
        P(("days", "chan"), None),
    )
    bands = mesh.shape["tm"] * mesh.shape["freq"]

    def step(recording, trailing, whiten_filter, pair_list):
        tables = band_tables(bands, 2 * trailing.shape[1])
        return jax.shard_map(
            functools.partial(local, tables),
            mesh=mesh,
            in_specs=placed,
            out_specs=P(("days", "chan"), None, ("tm", "freq"), None, None, None),
            check_vma=False,
        )(recording, trailing, whiten_filter, pair_list)

    return step
```

```python
import functools
import math

import jax
import jax.numpy as jnp
import ml_dtypes
import numpy as np
from jax import lax
from jax.experimental import pallas as pl
from jax.experimental.pallas import tpu as pltpu
from jax.sharding import PartitionSpec as P

FB = 512
REACH = 3
SLOTS = 4
LANES = 128


def band_tables(bands, length):
    samples = np.arange(length, dtype=np.int64)[:, None]
    bins = np.arange(FB, dtype=np.int64)[None, :]
    phase = (samples * bins % length).astype(np.float32)
    angle = np.float32(2.0 * math.pi / length) * phase
    ramp = np.float32(2.0 * math.pi / length) * np.arange(length, dtype=np.float32)
    taper = (np.float32(0.5) - np.float32(0.5) * np.cos(ramp))[:, None]
    normaliser = np.float32(1.0 / math.sqrt(0.375 * length))
    cosine = (taper * np.cos(angle) * normaliser).astype(ml_dtypes.bfloat16)
    sine = (-taper * np.sin(angle) * normaliser).astype(ml_dtypes.bfloat16)
    both = np.stack([cosine, sine], axis=1).reshape(length, 2, bands, FB // bands)
    return np.ascontiguousarray(both.transpose(2, 0, 1, 3)).reshape(bands, length, 2 * FB // bands)


def swapped(value, axis):
    return lax.ppermute(value, axis, [(0, 1), (1, 0)])


def block_of(own, other):
    low = lax.axis_index("freq") == 0
    a, b = own[...], other[...]
    return jnp.concatenate([jnp.where(low, a, b), jnp.where(low, b, a)], axis=0)


def hop_part(place, segment, value, table):
    hop = value.shape[1]
    half = place - segment
    start = pl.multiple_of(jnp.clip(half, 0, 1) * hop, hop)
    product = jnp.dot(value, table[pl.ds(start, hop), :], preferred_element_type=jnp.float32)
    return jnp.where((half == 0) | (half == 1), product, 0.0)


def begin_kernel(own, other, other_next, tables, total, table, sems):
    span = lax.axis_index("tm")
    band = span * lax.axis_size("freq") + lax.axis_index("freq")
    copy = pltpu.make_async_copy(tables.at[band], table, sems.at[0])
    copy.start()
    width = table.shape[1]
    segments = total.shape[1] // width
    mine = block_of(own.at[0], other)
    following = block_of(own.at[1], other_next)
    copy.wait()
    for segment in range(segments):
        value = hop_part(span, segment, mine, table)
        if segment == segments - 1:
            value += hop_part(segments, segment, following, table)
        total[:, segment * width : (segment + 1) * width] = value


def finish_kernel(spans, *refs):
    own, refs = refs[: spans - 1], refs[spans - 1 :]
    other, (table, begun, out) = refs[: spans - 1], refs[spans - 1 :]
    width = table.shape[1]
    blocks = [block_of(a, b) for a, b in zip(own, other)]
    for segment in range(spans):
        columns = slice(segment * width, (segment + 1) * width)
        value = begun[:, columns]
        for step in range(1, spans):
            place = lax.rem(lax.axis_index("tm") - step + spans, spans)
            value += hop_part(place, segment, blocks[step - 1], table)
        out[:, columns] = value.astype(jnp.bfloat16)


def band_kernel(chain, *refs):
    *weights, out = refs
    blocks, rows, width = out.shape
    here = lax.axis_index("chan")
    low = lax.axis_index("freq") == 0
    for block in range(blocks):
        if chain == 4:
            own, other = (ref[block].astype(jnp.float32) for ref in weights)
            place = jnp.bitwise_xor(here, block)
            tile = jnp.concatenate([jnp.where(low, own, other), jnp.where(low, other, own)], axis=1).T
        else:
            place = block
            tile = weights[0][block * rows : (block + 1) * rows, :].astype(jnp.float32)
        blank = jnp.zeros((rows, width - tile.shape[1]), jnp.float32)
        wide = jnp.concatenate([tile, blank], axis=1)
        out[place] = pltpu.roll(wide, 0, 1, stride=1, stride_axis=0).astype(jnp.bfloat16)


def cross_kernel(chain, segments, scaling, slots, *refs):
    here = lax.axis_index("chan")
    if chain == 4:
        raw, first, second, third, fourth, band, *refs = refs
        pick = lambda a, b, c, d: jnp.where(here == 0, a, jnp.where(here == 1, b, jnp.where(here == 2, c, d)))
        inner = (here == 1) | (here == 2)
        blocks = [
            (here, raw[...]),
            (pick(1, 3, 0, 2), first[...]),
            (pick(2, 0, 3, 1), second[...]),
            (pick(3, 2, 1, 0), jnp.where(inner, third[...], fourth[...])),
        ]
        edges = None
        mine, base = here, 0
    else:
        near = [0] + [d for d in range(-REACH, REACH + 1) if d]
        blocks = [(d + REACH, ref[...]) for d, ref in zip(near, refs)]
        refs = refs[len(near) :]
        before, after, band, *refs = refs
        edges = (before[...], after[...])
        mine, base = REACH, here - REACH
    out, padded, spectra, left, result, sems = refs
    rows, columns = left.shape[0] // 2, left.shape[1]
    count = len(blocks)
    rim = (padded.shape[0] - count * rows) // 4
    edge = count * rows + rim

    nothing = jnp.zeros((rim, columns), jnp.bfloat16)
    padded[:rim, :] = edges[0] if edges else nothing
    padded[edge : edge + rim, :] = edges[1] if edges else nothing
    padded[edge + rim :, :] = jnp.zeros((2 * rim, columns), jnp.bfloat16)
    for place, value in blocks:
        padded[pl.ds(pl.multiple_of(place * rows + rim, rim), rows), :] = value

    for block in range(count):
        start = block * rows
        matrix = band[block]
        window = padded[start : start + matrix.shape[1], :]
        predicted = jnp.dot(matrix, window, preferred_element_type=jnp.float32)
        raw = padded[start + rim : start + rim + rows, :].astype(jnp.float32)
        spectra[block] = (raw - predicted).astype(jnp.bfloat16)

    own = spectra[mine]
    left[:rows, :] = own
    half = columns // (2 * segments)
    turned = []
    for segment in range(segments):
        start = 2 * segment * half
        turned += [own[:, start + half : start + 2 * half], -own[:, start : start + half]]
    left[rows:, :] = jnp.concatenate(turned, axis=1)

    contract = (((1,), (1,)), ((), ()))
    for slot in range(SLOTS):
        partner = slots[0, slot]
        theirs = spectra[jnp.clip(partner - base, 0, count - 1)]
        both = lax.dot_general(left[...], theirs, contract, preferred_element_type=jnp.float32)
        both = jnp.where(partner >= 0, both * scaling, 0.0)
        result[slot, 0] = both[:rows]
        result[slot, 1] = both[rows:]
        pltpu.make_async_copy(result.at[slot], out.at[slot], sems.at[slot]).start()
    for slot in range(SLOTS):
        pltpu.make_async_copy(result.at[slot], out.at[slot], sems.at[slot]).wait()


def local(tables, recording, trailing, whiten_filter, pair_list):
    rows, hop = recording.shape
    spans, halves, chain = (lax.axis_size(axis) for axis in ("tm", "freq", "chan"))
    bands = spans * halves
    bins2 = 2 * FB // bands
    block_rows = halves * rows
    taps = whiten_filter.shape[1]
    rim = taps // 2
    here = lax.axis_index("chan")

    in_vmem = pl.BlockSpec(memory_space=pltpu.VMEM)
    small = pltpu.CompilerParams(vmem_limit_bytes=16 * 2**20)

    received = [
        lax.ppermute(recording, "tm", [(i, (i + step) % spans) for i in range(spans)])
        for step in range(1, spans)
    ]
    if chain == 4:
        filters = [
            lax.ppermute(whiten_filter.T, "chan", [(i, i ^ step) for i in range(chain)])
            for step in range(1, chain)
        ]
    else:
        filters = [lax.all_gather(whiten_filter, ("chan", "freq"), axis=0, tiled=True)]
    own = jnp.stack([recording, trailing])
    total = (block_rows, spans * bins2)
    in_hbm = pl.BlockSpec(memory_space=pltpu.HBM)
    begun, table = pl.pallas_call(
        begin_kernel,
        out_shape=[
            jax.ShapeDtypeStruct(total, jnp.float32),
            jax.ShapeDtypeStruct(tables.shape[1:], jnp.bfloat16),
        ],
        in_specs=[in_vmem, in_vmem, in_vmem, in_hbm],
        out_specs=[in_vmem, in_vmem],
        scratch_shapes=[pltpu.SemaphoreType.DMA((1,))],
        compiler_params=pltpu.CompilerParams(vmem_limit_bytes=48 * 2**20),
        name="begin_transform",
    )(own, swapped(recording, "freq"), swapped(trailing, "freq"), jnp.asarray(tables))
    received, filters, begun = lax.optimization_barrier((received, filters, begun))
    raw = pl.pallas_call(
        functools.partial(finish_kernel, spans),
        out_shape=jax.ShapeDtypeStruct(total, jnp.bfloat16),
        in_specs=[in_vmem] * (2 * spans),
        out_specs=in_vmem,
        compiler_params=small,
        name="finish_transform",
    )(*received, *(swapped(value, "freq") for value in received), table, begun)

    if chain == 4:
        near = chain
        weights = jnp.stack([whiten_filter.T, *filters])
        weights = (weights, swapped(weights, "freq"))
    else:
        near = 2 * REACH + 1
        beyond = jnp.pad(filters[0], ((REACH * block_rows, REACH * block_rows), (0, 0)))
        weights = (lax.dynamic_slice_in_dim(beyond, here * block_rows, near * block_rows, 0),)
    window = -(-(block_rows + taps) // LANES) * LANES
    band = pl.pallas_call(
        functools.partial(band_kernel, chain),
        out_shape=jax.ShapeDtypeStruct((near, block_rows, window), jnp.bfloat16),
        in_specs=[in_vmem] * len(weights),
        out_specs=in_vmem,
        compiler_params=small,
        name="band_matrix",
    )(*weights)

    if chain == 4:
        first = lax.ppermute(raw, "chan", [(0, 2), (2, 3), (3, 1), (1, 0)])
        second = lax.ppermute(raw, "chan", [(1, 3), (3, 2), (2, 0), (0, 1)])
        first, late = lax.optimization_barrier((first, raw))
        third = lax.ppermute(late, "chan", [(1, 2), (2, 1)])
        fourth = lax.ppermute(first, "chan", [(2, 3), (1, 0)])
        blocks = [raw, first, second, third, fourth]
    else:

        def shifted(value, distance):
            route = [(i - distance, i) for i in range(chain) if 0 <= i - distance < chain]
            return lax.ppermute(value, "chan", route)

        blocks = [raw]
        blocks += [shifted(raw, -d) for d in range(-REACH, REACH + 1) if d]
        blocks.append(shifted(raw[block_rows - rim :, :], REACH + 1))
        blocks.append(shifted(raw[:rim, :], -REACH - 1))

    out_shape = (SLOTS, 2, block_rows, block_rows)
    result = pl.pallas_call(
        functools.partial(cross_kernel, chain, spans, 1.0 / math.sqrt(spans * bins2 // 2)),
        out_shape=jax.ShapeDtypeStruct(out_shape, jnp.float32),
        in_specs=[pl.BlockSpec(memory_space=pltpu.SMEM)] + [in_vmem] * (len(blocks) + 1),
        out_specs=in_hbm,
        scratch_shapes=[
            pltpu.VMEM((near * block_rows + 4 * rim, total[1]), jnp.bfloat16),
            pltpu.VMEM((near, *total), jnp.bfloat16),
            pltpu.VMEM((2 * block_rows, total[1]), jnp.bfloat16),
            pltpu.VMEM(out_shape, jnp.float32),
            pltpu.SemaphoreType.DMA((SLOTS,)),
        ],
        compiler_params=pltpu.CompilerParams(vmem_limit_bytes=24 * 2**20),
        name="cross",
    )(pair_list, *blocks, band)
    return result.reshape(1, SLOTS, 1, 2, block_rows, block_rows)


def solution(mesh):
    placed = (
        P(("days", "chan", "freq"), "tm"),
        P(("days", "chan", "freq"), None),
        P(("chan", "freq"), None),
        P(("days", "chan"), None),
    )
    bands = mesh.shape["tm"] * mesh.shape["freq"]

    def step(recording, trailing, whiten_filter, pair_list):
        tables = band_tables(bands, 2 * trailing.shape[1])
        return jax.shard_map(
            functools.partial(local, tables),
            mesh=mesh,
            in_specs=placed,
            out_specs=P(("days", "chan"), None, ("tm", "freq"), None, None, None),
            check_vma=False,
        )(recording, trailing, whiten_filter, pair_list)

    return step
```

```python
import functools
import math

import jax
import jax.numpy as jnp
import ml_dtypes
import numpy as np
from jax import lax
from jax.experimental import pallas as pl
from jax.experimental.pallas import tpu as pltpu
from jax.sharding import PartitionSpec as P

FB = 512
REACH = 3
SLOTS = 4
LANES = 128


def band_tables(spans, halves, length):
    samples = np.arange(length, dtype=np.int64)[:, None]
    bins = np.arange(FB, dtype=np.int64)[None, :]
    phase = (samples * bins % length).astype(np.float32)
    angle = np.float32(2.0 * math.pi / length) * phase
    ramp = np.float32(2.0 * math.pi / length) * np.arange(length, dtype=np.float32)
    taper = (np.float32(0.5) - np.float32(0.5) * np.cos(ramp))[:, None]
    normaliser = np.float32(1.0 / math.sqrt(0.375 * length))
    cosine = (taper * np.cos(angle) * normaliser).astype(ml_dtypes.bfloat16)
    sine = (-taper * np.sin(angle) * normaliser).astype(ml_dtypes.bfloat16)
    both = np.stack([cosine, sine], axis=1).reshape(length, 2, spans, halves, -1)
    return np.ascontiguousarray(both.transpose(2, 0, 3, 1, 4)).reshape(spans, length, -1)


def swapped(value, axis):
    return lax.ppermute(value, axis, [(0, 1), (1, 0)])


def block_of(own, other):
    low = lax.axis_index("freq") == 0
    a, b = own[...], other[...]
    return jnp.concatenate([jnp.where(low, a, b), jnp.where(low, b, a)], axis=0)


def hop_part(place, segment, value, table):
    hop = value.shape[1]
    half = place - segment
    start = pl.multiple_of(jnp.clip(half, 0, 1) * hop, hop)
    product = jnp.dot(value, table[pl.ds(start, hop), :], preferred_element_type=jnp.float32)
    return jnp.where((half == 0) | (half == 1), product, 0.0)


def begin_kernel(own, tables, total, table, sems):
    span = lax.axis_index("tm")
    copy = pltpu.make_async_copy(tables.at[span], table, sems.at[0])
    copy.start()
    width = table.shape[1]
    segments = total.shape[1] // width
    copy.wait()
    for segment in range(segments):
        value = hop_part(span, segment, own[0], table)
        if segment == segments - 1:
            value += hop_part(segments, segment, own[1], table)
        total[:, segment * width : (segment + 1) * width] = value


def finish_kernel(spans, *refs):
    hops, (table, begun, mine, theirs) = refs[: spans - 1], refs[spans - 1 :]
    width = table.shape[1]
    part = width // 2
    low = lax.axis_index("freq") == 0
    for segment in range(spans):
        value = begun[:, segment * width : (segment + 1) * width]
        for step in range(1, spans):
            place = lax.rem(lax.axis_index("tm") - step + spans, spans)
            value += hop_part(place, segment, hops[step - 1][...], table)
        first, second = value[:, :part].astype(jnp.bfloat16), value[:, part:].astype(jnp.bfloat16)
        columns = slice(segment * part, (segment + 1) * part)
        mine[:, columns] = jnp.where(low, first, second)
        theirs[:, columns] = jnp.where(low, second, first)


def block_kernel(own, other, out):
    out[...] = block_of(own, other)


def band_kernel(chain, *refs):
    *weights, out = refs
    blocks, rows, width = out.shape
    here = lax.axis_index("chan")
    low = lax.axis_index("freq") == 0
    for block in range(blocks):
        if chain == 4:
            own, other = (ref[block].astype(jnp.float32) for ref in weights)
            place = jnp.bitwise_xor(here, block)
            tile = jnp.concatenate([jnp.where(low, own, other), jnp.where(low, other, own)], axis=1).T
        else:
            place = block
            tile = weights[0][block * rows : (block + 1) * rows, :].astype(jnp.float32)
        blank = jnp.zeros((rows, width - tile.shape[1]), jnp.float32)
        wide = jnp.concatenate([tile, blank], axis=1)
        out[place] = pltpu.roll(wide, 0, 1, stride=1, stride_axis=0).astype(jnp.bfloat16)


def whitened(band, window, raw):
    predicted = jnp.dot(band, window, preferred_element_type=jnp.float32)
    return (raw.astype(jnp.float32) - predicted).astype(jnp.bfloat16)


def pair_products(slots, spectra, mine, base, segments, scaling, out, left, result, sems):
    count, rows, columns = spectra.shape
    own = spectra[mine]
    left[:rows, :] = own
    half = columns // (2 * segments)
    turned = []
    for segment in range(segments):
        start = 2 * segment * half
        turned += [own[:, start + half : start + 2 * half], -own[:, start : start + half]]
    left[rows:, :] = jnp.concatenate(turned, axis=1)

    contract = (((1,), (1,)), ((), ()))
    for slot in range(SLOTS):
        partner = slots[0, slot]
        theirs = spectra[jnp.clip(partner - base, 0, count - 1)]
        both = lax.dot_general(left[...], theirs, contract, preferred_element_type=jnp.float32)
        both = jnp.where(partner >= 0, both * scaling, 0.0)
        result[slot, 0] = both[:rows]
        result[slot, 1] = both[rows:]
        pltpu.make_async_copy(result.at[slot], out.at[slot], sems.at[slot]).start()
    for slot in range(SLOTS):
        pltpu.make_async_copy(result.at[slot], out.at[slot], sems.at[slot]).wait()


def cross_kernel(segments, scaling, slots, *refs):
    near = [0] + [d for d in range(-REACH, REACH + 1) if d]
    blocks, (before, after, band, out, padded, spectra, left, result, sems) = refs[: len(near)], refs[len(near) :]
    count, rows, columns = spectra.shape
    rim = before.shape[0]
    edge = count * rows + rim
    padded[:rim, :] = before[...]
    padded[edge : edge + rim, :] = after[...]
    padded[edge + rim :, :] = jnp.zeros((padded.shape[0] - edge - rim, columns), jnp.bfloat16)
    for distance, value in zip(near, blocks):
        start = (distance + REACH) * rows + rim
        padded[start : start + rows, :] = value[...]
    for block in range(count):
        start = block * rows
        window = padded[start : start + band.shape[2], :]
        spectra[block] = whitened(band[block], window, padded[start + rim : start + rim + rows, :])
    base = lax.axis_index("chan") - REACH
    pair_products(slots, spectra, REACH, base, segments, scaling, out, left, result, sems)


def chosen(a, b, c, d):
    here = lax.axis_index("chan")
    return jnp.where(here == 0, a, jnp.where(here == 1, b, jnp.where(here == 2, c, d)))


def relay_kernel(raw, first, first_other, arrived, down, up):
    here = lax.axis_index("chan")
    value = block_of(first, first_other)
    arrived[...] = value
    down[...] = jnp.where(here == 1, value, raw[...])
    up[...] = jnp.where(here == 2, value, raw[...])


def early_kernel(raw, first, second, band, padded, spectra):
    count, rows, columns = spectra.shape
    rim = (padded.shape[0] - count * rows) // 4
    edge = count * rows + rim
    padded[:rim, :] = jnp.zeros((rim, columns), jnp.bfloat16)
    padded[edge:, :] = jnp.zeros((3 * rim, columns), jnp.bfloat16)
    last = chosen(3, 2, 1, 0)
    padded[pl.ds(pl.multiple_of(last * rows + rim, rim), rows), :] = jnp.zeros((rows, columns), jnp.bfloat16)
    for place, value in (
        (lax.axis_index("chan"), raw),
        (chosen(1, 3, 0, 2), first),
        (chosen(2, 0, 3, 1), second),
    ):
        padded[pl.ds(pl.multiple_of(place * rows + rim, rim), rows), :] = value[...]
    for block in range(count):
        start = block * rows
        window = padded[start : start + band.shape[2], :]
        spectra[block] = whitened(band[block], window, padded[start + rim : start + rim + rows, :])


def late_kernel(segments, scaling, slots, padded, early, third, fourth, band, out, spectra, left, result, sems):
    count, rows, columns = spectra.shape
    width = band.shape[2]
    rim = (padded.shape[0] - count * rows) // 4
    here = lax.axis_index("chan")
    last = chosen(3, 2, 1, 0)
    value = jnp.where(here <= 1, third[...], fourth[...])
    spectra[...] = early[...]

    start = pl.multiple_of(last * rows, rows)
    above = padded[pl.ds(start, rim), :]
    below = padded[pl.ds(start + rim + rows, width - rim - rows), :]
    window = jnp.concatenate([above, value, below], axis=0)
    spectra[last] = whitened(band[last], window, value)

    @pl.when(last > 0)
    def _():
        block = last - 1
        half = rows // 2
        upper = padded[pl.ds(pl.multiple_of(start - half, half), half + rim), :]
        window = jnp.concatenate([upper, value[: width - rows - rim]], axis=0)
        strip = whitened(band[block, rows - rim :, half:], window, above)
        spectra[block, rows - rim :, :] = strip

    @pl.when(last < count - 1)
    def _():
        block = last + 1
        lower = padded[pl.ds(start + rows + rim, LANES - rim), :]
        window = jnp.concatenate([value[rows - rim :], lower], axis=0)
        strip = whitened(band[block, :rim, :LANES], window, lower[:rim])
        spectra[block, :rim, :] = strip

    pair_products(slots, spectra, here, 0, segments, scaling, out, left, result, sems)


def local(tables, recording, trailing, whiten_filter, pair_list):
    rows, hop = recording.shape
    spans, halves, chain = (lax.axis_size(axis) for axis in ("tm", "freq", "chan"))
    bands = spans * halves
    bins2 = 2 * FB // bands
    block_rows = halves * rows
    taps = whiten_filter.shape[1]
    rim = taps // 2
    here = lax.axis_index("chan")

    in_vmem = pl.BlockSpec(memory_space=pltpu.VMEM)
    small = pltpu.CompilerParams(vmem_limit_bytes=16 * 2**20)

    received = [
        lax.ppermute(recording, "tm", [(i, (i + step) % spans) for i in range(spans)])
        for step in range(1, spans)
    ]
    if chain == 4:
        filters = [
            lax.ppermute(whiten_filter.T, "chan", [(i, i ^ step) for i in range(chain)])
            for step in range(1, chain)
        ]
    else:
        filters = [lax.all_gather(whiten_filter, ("chan", "freq"), axis=0, tiled=True)]
    own = jnp.stack([recording, trailing])
    total = (block_rows, spans * bins2)
    in_hbm = pl.BlockSpec(memory_space=pltpu.HBM)
    begun, table = pl.pallas_call(
        begin_kernel,
        out_shape=[
            jax.ShapeDtypeStruct((rows, halves * total[1]), jnp.float32),
            jax.ShapeDtypeStruct(tables.shape[1:], jnp.bfloat16),
        ],
        in_specs=[in_vmem, in_hbm],
        out_specs=[in_vmem, in_vmem],
        scratch_shapes=[pltpu.SemaphoreType.DMA((1,))],
        compiler_params=pltpu.CompilerParams(vmem_limit_bytes=48 * 2**20),
        name="begin_transform",
    )(own, jnp.asarray(tables))
    received, filters, begun = lax.optimization_barrier((received, filters, begun))
    half_rows = (rows, total[1])
    mine, theirs = pl.pallas_call(
        functools.partial(finish_kernel, spans),
        out_shape=[jax.ShapeDtypeStruct(half_rows, jnp.bfloat16)] * 2,
        in_specs=[in_vmem] * (spans + 1),
        out_specs=[in_vmem] * 2,
        compiler_params=small,
        name="finish_transform",
    )(*received, table, begun)
    raw = pl.pallas_call(
        block_kernel,
        out_shape=jax.ShapeDtypeStruct(total, jnp.bfloat16),
        in_specs=[in_vmem] * 2,
        out_specs=in_vmem,
        compiler_params=small,
        name="block",
    )(mine, swapped(theirs, "freq"))

    if chain == 4:
        near = chain
        weights = jnp.stack([whiten_filter.T, *filters])
        weights = (weights, swapped(weights, "freq"))
    else:
        near = 2 * REACH + 1
        beyond = jnp.pad(filters[0], ((REACH * block_rows, REACH * block_rows), (0, 0)))
        weights = (lax.dynamic_slice_in_dim(beyond, here * block_rows, near * block_rows, 0),)
    window = -(-(block_rows + taps) // LANES) * LANES
    band = pl.pallas_call(
        functools.partial(band_kernel, chain),
        out_shape=jax.ShapeDtypeStruct((near, block_rows, window), jnp.bfloat16),
        in_specs=[in_vmem] * len(weights),
        out_specs=in_vmem,
        compiler_params=small,
        name="band_matrix",
    )(*weights)

    if chain == 4:
        route = [(0, 2), (2, 3), (3, 1), (1, 0)]
        first = lax.ppermute(mine, "chan", route)
        across = [(2 * i + half, 2 * j + 1 - half) for i, j in route for half in range(2)]
        first_other = lax.ppermute(theirs, ("chan", "freq"), across)
        second = lax.ppermute(raw, "chan", [(1, 3), (3, 2), (2, 0), (0, 1)])
        first, down, up = pl.pallas_call(
            relay_kernel,
            out_shape=[jax.ShapeDtypeStruct(total, jnp.bfloat16)] * 3,
            in_specs=[in_vmem] * 3,
            out_specs=[in_vmem] * 3,
            compiler_params=small,
            name="relay",
        )(raw, first, first_other)
        third = lax.ppermute(down, "chan", [(1, 0), (2, 1)])
        fourth = lax.ppermute(up, "chan", [(2, 3), (1, 2)])
    else:

        def shifted(value, distance):
            route = [(i - distance, i) for i in range(chain) if 0 <= i - distance < chain]
            return lax.ppermute(value, "chan", route)

        blocks = [raw]
        blocks += [shifted(raw, -d) for d in range(-REACH, REACH + 1) if d]
        blocks.append(shifted(raw[block_rows - rim :, :], REACH + 1))
        blocks.append(shifted(raw[:rim, :], -REACH - 1))

    padded = (near * block_rows + 4 * rim, total[1])
    spectra = (near, *total)
    if chain == 4:
        operands = pl.pallas_call(
            early_kernel,
            out_shape=[jax.ShapeDtypeStruct(shape, jnp.bfloat16) for shape in (padded, spectra)],
            in_specs=[in_vmem] * 4,
            out_specs=[in_vmem] * 2,
            compiler_params=small,
            name="early_whitening",
        )(raw, first, second, band)
        operands = (*operands, third, fourth, band)
        kernel, scratch = late_kernel, []
    else:
        operands = (*blocks, band)
        kernel, scratch = cross_kernel, [pltpu.VMEM(padded, jnp.bfloat16)]
    out_shape = (SLOTS, 2, block_rows, block_rows)
    result = pl.pallas_call(
        functools.partial(kernel, spans, 1.0 / math.sqrt(spans * bins2 // 2)),
        out_shape=jax.ShapeDtypeStruct(out_shape, jnp.float32),
        in_specs=[pl.BlockSpec(memory_space=pltpu.SMEM)] + [in_vmem] * len(operands),
        out_specs=in_hbm,
        scratch_shapes=[
            *scratch,
            pltpu.VMEM(spectra, jnp.bfloat16),
            pltpu.VMEM((2 * block_rows, total[1]), jnp.bfloat16),
            pltpu.VMEM(out_shape, jnp.float32),
            pltpu.SemaphoreType.DMA((SLOTS,)),
        ],
        compiler_params=pltpu.CompilerParams(vmem_limit_bytes=24 * 2**20),
        name="cross",
    )(pair_list, *operands)
    return result.reshape(1, SLOTS, 1, 2, block_rows, block_rows)


def solution(mesh):
    placed = (
        P(("days", "chan", "freq"), "tm"),
        P(("days", "chan", "freq"), None),
        P(("chan", "freq"), None),
        P(("days", "chan"), None),
    )

    def step(recording, trailing, whiten_filter, pair_list):
        tables = band_tables(mesh.shape["tm"], mesh.shape["freq"], 2 * trailing.shape[1])
        return jax.shard_map(
            functools.partial(local, tables),
            mesh=mesh,
            in_specs=placed,
            out_specs=P(("days", "chan"), None, ("tm", "freq"), None, None, None),
            check_vma=False,
        )(recording, trailing, whiten_filter, pair_list)

    return step
```

```python
import functools
import math

import jax
import jax.numpy as jnp
import ml_dtypes
import numpy as np
from jax import lax
from jax.experimental import pallas as pl
from jax.experimental.pallas import tpu as pltpu
from jax.sharding import PartitionSpec as P

FB = 512
REACH = 3
SLOTS = 4
LANES = 128


def band_tables(spans, halves, length):
    samples = np.arange(length, dtype=np.int64)[:, None]
    bins = np.arange(FB, dtype=np.int64)[None, :]
    phase = (samples * bins % length).astype(np.float32)
    angle = np.float32(2.0 * math.pi / length) * phase
    ramp = np.float32(2.0 * math.pi / length) * np.arange(length, dtype=np.float32)
    taper = (np.float32(0.5) - np.float32(0.5) * np.cos(ramp))[:, None]
    normaliser = np.float32(1.0 / math.sqrt(0.375 * length))
    cosine = (taper * np.cos(angle) * normaliser).astype(ml_dtypes.bfloat16)
    sine = (-taper * np.sin(angle) * normaliser).astype(ml_dtypes.bfloat16)
    both = np.stack([cosine, sine], axis=1).reshape(length, 2, spans, halves, -1)
    return np.ascontiguousarray(both.transpose(2, 0, 3, 1, 4)).reshape(spans, length, -1)


def swapped(value, axis):
    return lax.ppermute(value, axis, [(0, 1), (1, 0)])


def block_of(own, other):
    low = lax.axis_index("freq") == 0
    a, b = own[...], other[...]
    return jnp.concatenate([jnp.where(low, a, b), jnp.where(low, b, a)], axis=0)


def hop_part(place, segment, value, table):
    hop = value.shape[1]
    half = place - segment
    start = pl.multiple_of(jnp.clip(half, 0, 1) * hop, hop)
    product = jnp.dot(value, table[pl.ds(start, hop), :], preferred_element_type=jnp.float32)
    return jnp.where((half == 0) | (half == 1), product, 0.0)


def begin_kernel(recording, trailing, tables, total, table, hop, following, sems):
    span = lax.axis_index("tm")
    copies = [
        pltpu.make_async_copy(source, target, sems.at[index])
        for index, (source, target) in enumerate(
            ((recording, hop), (trailing, following), (tables.at[span], table))
        )
    ]
    for copy in copies:
        copy.start()
    for copy in copies:
        copy.wait()
    width = table.shape[1]
    segments = total.shape[1] // width
    for segment in range(segments):
        value = hop_part(span, segment, hop[...], table)
        if segment == segments - 1:
            value += hop_part(segments, segment, following[...], table)
        total[:, segment * width : (segment + 1) * width] = value


def finish_kernel(spans, *refs):
    hops, (table, begun, mine, theirs) = refs[: spans - 1], refs[spans - 1 :]
    width = table.shape[1]
    part = width // 2
    low = lax.axis_index("freq") == 0
    for segment in range(spans):
        value = begun[:, segment * width : (segment + 1) * width]
        for step in range(1, spans):
            place = lax.rem(lax.axis_index("tm") - step + spans, spans)
            value += hop_part(place, segment, hops[step - 1][...], table)
        first, second = value[:, :part].astype(jnp.bfloat16), value[:, part:].astype(jnp.bfloat16)
        columns = slice(segment * part, (segment + 1) * part)
        mine[:, columns] = jnp.where(low, first, second)
        theirs[:, columns] = jnp.where(low, second, first)


def block_kernel(own, other, out):
    out[...] = block_of(own, other)


def band_kernel(chain, *refs):
    *weights, out = refs
    blocks, rows, width = out.shape
    here = lax.axis_index("chan")
    low = lax.axis_index("freq") == 0
    for block in range(blocks):
        if chain == 4:
            own, other = (ref[block].astype(jnp.float32) for ref in weights)
            place = jnp.bitwise_xor(here, block)
            tile = jnp.concatenate([jnp.where(low, own, other), jnp.where(low, other, own)], axis=1).T
        else:
            place = block
            tile = weights[0][block * rows : (block + 1) * rows, :].astype(jnp.float32)
        blank = jnp.zeros((rows, width - tile.shape[1]), jnp.float32)
        wide = jnp.concatenate([tile, blank], axis=1)
        out[place] = pltpu.roll(wide, 0, 1, stride=1, stride_axis=0).astype(jnp.bfloat16)


def whitened(band, window, raw):
    predicted = jnp.dot(band, window, preferred_element_type=jnp.float32)
    return (raw.astype(jnp.float32) - predicted).astype(jnp.bfloat16)


def pair_products(slots, own, spectra_of, segments, scaling, out, left, result, sems):
    rows, columns = own.shape
    left[:rows, :] = own
    half = columns // (2 * segments)
    turned = []
    for segment in range(segments):
        start = 2 * segment * half
        turned += [own[:, start + half : start + 2 * half], -own[:, start : start + half]]
    left[rows:, :] = jnp.concatenate(turned, axis=1)

    contract = (((1,), (1,)), ((), ()))
    for slot in range(SLOTS):
        partner = slots[0, slot]
        theirs = spectra_of(jnp.maximum(partner, 0))
        both = lax.dot_general(left[...], theirs, contract, preferred_element_type=jnp.float32)
        both = jnp.where(partner >= 0, both * scaling, 0.0)
        result[slot, 0] = both[:rows]
        result[slot, 1] = both[rows:]
        pltpu.make_async_copy(result.at[slot], out.at[slot], sems.at[slot]).start()
    for slot in range(SLOTS):
        pltpu.make_async_copy(result.at[slot], out.at[slot], sems.at[slot]).wait()


def cross_kernel(segments, scaling, slots, *refs):
    near = [0] + [d for d in range(-REACH, REACH + 1) if d]
    blocks, (before, after, band, out, padded, spectra, left, result, sems) = refs[: len(near)], refs[len(near) :]
    count, rows, columns = spectra.shape
    rim = before.shape[0]
    edge = count * rows + rim
    padded[:rim, :] = before[...]
    padded[edge : edge + rim, :] = after[...]
    padded[edge + rim :, :] = jnp.zeros((padded.shape[0] - edge - rim, columns), jnp.bfloat16)
    for distance, value in zip(near, blocks):
        start = (distance + REACH) * rows + rim
        padded[start : start + rows, :] = value[...]
    for block in range(count):
        start = block * rows
        window = padded[start : start + band.shape[2], :]
        spectra[block] = whitened(band[block], window, padded[start + rim : start + rim + rows, :])
    base = lax.axis_index("chan") - REACH
    spectra_of = lambda block: spectra[jnp.clip(block - base, 0, count - 1)]
    pair_products(slots, spectra[REACH], spectra_of, segments, scaling, out, left, result, sems)


def chosen(a, b, c, d):
    here = lax.axis_index("chan")
    return jnp.where(here == 0, a, jnp.where(here == 1, b, jnp.where(here == 2, c, d)))


def relay_kernel(raw, first, first_other, arrived, down, up):
    here = lax.axis_index("chan")
    value = block_of(first, first_other)
    arrived[...] = value
    down[...] = jnp.where(here == 1, value, raw[...])
    up[...] = jnp.where(here == 2, value, raw[...])


def early_kernel(raw, first, second, band, padded, spectra):
    count, rows, columns = spectra.shape
    rim = (padded.shape[0] - count * rows) // 4
    edge = count * rows + rim
    padded[:rim, :] = jnp.zeros((rim, columns), jnp.bfloat16)
    padded[edge:, :] = jnp.zeros((3 * rim, columns), jnp.bfloat16)
    last = chosen(3, 2, 1, 0)
    padded[pl.ds(pl.multiple_of(last * rows + rim, rim), rows), :] = jnp.zeros((rows, columns), jnp.bfloat16)
    for place, value in (
        (lax.axis_index("chan"), raw),
        (chosen(1, 3, 0, 2), first),
        (chosen(2, 0, 3, 1), second),
    ):
        padded[pl.ds(pl.multiple_of(place * rows + rim, rim), rows), :] = value[...]
    for block in range(count):
        start = block * rows
        window = padded[start : start + band.shape[2], :]
        spectra[block] = whitened(band[block], window, padded[start + rim : start + rim + rows, :])


def late_kernel(segments, scaling, slots, padded, early, third, fourth, band, out, left, result, sems):
    count, rows, columns = early.shape
    width = band.shape[2]
    rim = (padded.shape[0] - count * rows) // 4
    here = lax.axis_index("chan")
    last = chosen(3, 2, 1, 0)
    value = jnp.where(here <= 1, third[...], fourth[...])

    start = pl.multiple_of(last * rows, rows)
    above = padded[pl.ds(start, rim), :]
    below = padded[pl.ds(start + rim + rows, width - rim - rows), :]
    window = jnp.concatenate([above, value, below], axis=0)
    arrived = whitened(band[last], window, value)

    half = rows // 2
    upper = padded[pl.ds(pl.multiple_of(jnp.maximum(start - half, 0), half), half + rim), :]
    window = jnp.concatenate([upper, value[: width - rows - rim]], axis=0)
    bottom = whitened(band[jnp.maximum(last - 1, 0), rows - rim :, half:], window, above)
    lower = below[: LANES - rim]
    window = jnp.concatenate([value[rows - rim :], lower], axis=0)
    top = whitened(band[jnp.minimum(last + 1, count - 1), :rim, :LANES], window, lower[:rim])

    def spectra_of(block):
        known = jnp.where(block == last, arrived, early[block])
        return jnp.concatenate(
            [
                jnp.where(block == last + 1, top, known[:rim]),
                known[rim : rows - rim],
                jnp.where(block == last - 1, bottom, known[rows - rim :]),
            ],
            axis=0,
        )

    pair_products(slots, spectra_of(here), spectra_of, segments, scaling, out, left, result, sems)


def local(tables, recording, trailing, whiten_filter, pair_list):
    rows, hop = recording.shape
    spans, halves, chain = (lax.axis_size(axis) for axis in ("tm", "freq", "chan"))
    bands = spans * halves
    bins2 = 2 * FB // bands
    block_rows = halves * rows
    taps = whiten_filter.shape[1]
    rim = taps // 2
    here = lax.axis_index("chan")

    in_vmem = pl.BlockSpec(memory_space=pltpu.VMEM)
    small = pltpu.CompilerParams(vmem_limit_bytes=16 * 2**20)

    received = [
        lax.ppermute(recording, "tm", [(i, (i + step) % spans) for i in range(spans)])
        for step in range(1, spans)
    ]
    if chain == 4:
        filters = [
            lax.ppermute(whiten_filter.T, "chan", [(i, i ^ step) for i in range(chain)])
            for step in range(1, chain)
        ]
    else:
        filters = [lax.all_gather(whiten_filter, ("chan", "freq"), axis=0, tiled=True)]
    total = (block_rows, spans * bins2)
    in_hbm = pl.BlockSpec(memory_space=pltpu.HBM)
    begun, table = pl.pallas_call(
        begin_kernel,
        out_shape=[
            jax.ShapeDtypeStruct((rows, halves * total[1]), jnp.float32),
            jax.ShapeDtypeStruct(tables.shape[1:], jnp.bfloat16),
        ],
        in_specs=[in_hbm] * 3,
        out_specs=[in_vmem] * 2,
        scratch_shapes=[
            pltpu.VMEM(recording.shape, jnp.bfloat16),
            pltpu.VMEM(trailing.shape, jnp.bfloat16),
            pltpu.SemaphoreType.DMA((3,)),
        ],
        compiler_params=small,
        name="begin_transform",
    )(
        *(
            pltpu.with_memory_space_constraint(value, pltpu.HBM)
            for value in (recording, trailing, jnp.asarray(tables))
        )
    )
    received, filters, begun = lax.optimization_barrier((received, filters, begun))
    half_rows = (rows, total[1])
    mine, theirs = pl.pallas_call(
        functools.partial(finish_kernel, spans),
        out_shape=[jax.ShapeDtypeStruct(half_rows, jnp.bfloat16)] * 2,
        in_specs=[in_vmem] * (spans + 1),
        out_specs=[in_vmem] * 2,
        compiler_params=small,
        name="finish_transform",
    )(*received, table, begun)
    raw = pl.pallas_call(
        block_kernel,
        out_shape=jax.ShapeDtypeStruct(total, jnp.bfloat16),
        in_specs=[in_vmem] * 2,
        out_specs=in_vmem,
        compiler_params=small,
        name="block",
    )(mine, swapped(theirs, "freq"))

    if chain == 4:
        near = chain
        weights = jnp.stack([whiten_filter.T, *filters])
        weights = (weights, swapped(weights, "freq"))
    else:
        near = 2 * REACH + 1
        beyond = jnp.pad(filters[0], ((REACH * block_rows, REACH * block_rows), (0, 0)))
        weights = (lax.dynamic_slice_in_dim(beyond, here * block_rows, near * block_rows, 0),)
    window = -(-(block_rows + taps) // LANES) * LANES
    band = pl.pallas_call(
        functools.partial(band_kernel, chain),
        out_shape=jax.ShapeDtypeStruct((near, block_rows, window), jnp.bfloat16),
        in_specs=[in_vmem] * len(weights),
        out_specs=in_vmem,
        compiler_params=small,
        name="band_matrix",
    )(*weights)

    if chain == 4:
        route = [(0, 2), (2, 3), (3, 1), (1, 0)]
        first = lax.ppermute(mine, "chan", route)
        across = [(2 * i + half, 2 * j + 1 - half) for i, j in route for half in range(2)]
        first_other = lax.ppermute(theirs, ("chan", "freq"), across)
        second = lax.ppermute(raw, "chan", [(1, 3), (3, 2), (2, 0), (0, 1)])
        first, down, up = pl.pallas_call(
            relay_kernel,
            out_shape=[jax.ShapeDtypeStruct(total, jnp.bfloat16)] * 3,
            in_specs=[in_vmem] * 3,
            out_specs=[in_vmem] * 3,
            compiler_params=small,
            name="relay",
        )(raw, first, first_other)
        third = lax.ppermute(down, "chan", [(1, 0), (2, 1)])
        fourth = lax.ppermute(up, "chan", [(2, 3), (1, 2)])
    else:

        def shifted(value, distance):
            route = [(i - distance, i) for i in range(chain) if 0 <= i - distance < chain]
            return lax.ppermute(value, "chan", route)

        blocks = [raw]
        blocks += [shifted(raw, -d) for d in range(-REACH, REACH + 1) if d]
        blocks.append(shifted(raw[block_rows - rim :, :], REACH + 1))
        blocks.append(shifted(raw[:rim, :], -REACH - 1))

    padded = (near * block_rows + 4 * rim, total[1])
    spectra = (near, *total)
    if chain == 4:
        operands = pl.pallas_call(
            early_kernel,
            out_shape=[jax.ShapeDtypeStruct(shape, jnp.bfloat16) for shape in (padded, spectra)],
            in_specs=[in_vmem] * 4,
            out_specs=[in_vmem] * 2,
            compiler_params=small,
            name="early_whitening",
        )(raw, first, second, band)
        operands = (*operands, third, fourth, band)
        kernel, scratch = late_kernel, []
    else:
        operands = (*blocks, band)
        kernel, scratch = cross_kernel, [pltpu.VMEM(shape, jnp.bfloat16) for shape in (padded, spectra)]
    out_shape = (SLOTS, 2, block_rows, block_rows)
    result = pl.pallas_call(
        functools.partial(kernel, spans, 1.0 / math.sqrt(spans * bins2 // 2)),
        out_shape=jax.ShapeDtypeStruct(out_shape, jnp.float32),
        in_specs=[pl.BlockSpec(memory_space=pltpu.SMEM)] + [in_vmem] * len(operands),
        out_specs=in_hbm,
        scratch_shapes=[
            *scratch,
            pltpu.VMEM((2 * block_rows, total[1]), jnp.bfloat16),
            pltpu.VMEM(out_shape, jnp.float32),
            pltpu.SemaphoreType.DMA((SLOTS,)),
        ],
        compiler_params=pltpu.CompilerParams(vmem_limit_bytes=24 * 2**20),
        name="cross",
    )(pair_list, *operands)
    return result.reshape(1, SLOTS, 1, 2, block_rows, block_rows)


def solution(mesh):
    placed = (
        P(("days", "chan", "freq"), "tm"),
        P(("days", "chan", "freq"), None),
        P(("chan", "freq"), None),
        P(("days", "chan"), None),
    )

    def step(recording, trailing, whiten_filter, pair_list):
        tables = band_tables(mesh.shape["tm"], mesh.shape["freq"], 2 * trailing.shape[1])
        return jax.shard_map(
            functools.partial(local, tables),
            mesh=mesh,
            in_specs=placed,
            out_specs=P(("days", "chan"), None, ("tm", "freq"), None, None, None),
            check_vma=False,
        )(recording, trailing, whiten_filter, pair_list)

    return step
```

```python
import functools
import math

import jax
import jax.numpy as jnp
import ml_dtypes
import numpy as np
from jax import lax
from jax.experimental import pallas as pl
from jax.experimental.pallas import tpu as pltpu
from jax.sharding import PartitionSpec as P

FB = 512
REACH = 3
SLOTS = 4
LANES = 128


def band_tables(spans, halves, length):
    samples = np.arange(length, dtype=np.int64)[:, None]
    bins = np.arange(FB, dtype=np.int64)[None, :]
    phase = (samples * bins % length).astype(np.float32)
    angle = np.float32(2.0 * math.pi / length) * phase
    ramp = np.float32(2.0 * math.pi / length) * np.arange(length, dtype=np.float32)
    taper = (np.float32(0.5) - np.float32(0.5) * np.cos(ramp))[:, None]
    normaliser = np.float32(1.0 / math.sqrt(0.375 * length))
    cosine = (taper * np.cos(angle) * normaliser).astype(ml_dtypes.bfloat16)
    sine = (-taper * np.sin(angle) * normaliser).astype(ml_dtypes.bfloat16)
    both = np.stack([cosine, sine], axis=1).reshape(length, 2, spans, halves, -1)
    return np.ascontiguousarray(both.transpose(2, 0, 3, 1, 4)).reshape(spans, length, -1)


def swapped(value, axis):
    return lax.ppermute(value, axis, [(0, 1), (1, 0)])


def block_of(own, other):
    low = lax.axis_index("freq") == 0
    a, b = own[...], other[...]
    return jnp.concatenate([jnp.where(low, a, b), jnp.where(low, b, a)], axis=0)


def hop_parts(place, value, table, segments):
    hop = value.shape[1]
    first = jnp.dot(value, table[:hop, :], preferred_element_type=jnp.float32)
    second = jnp.dot(value, table[hop:, :], preferred_element_type=jnp.float32)
    for segment in range(segments):
        yield jnp.where(place == segment, first, jnp.where(place == segment + 1, second, 0.0))


def begin_kernel(recording, trailing, tables, total, table, hop, following, sems):
    span = lax.axis_index("tm")
    width = table.shape[1]
    segments = total.shape[1] // width
    size = hop.shape[1]
    copies = [
        pltpu.make_async_copy(source, target, sems.at[index])
        for index, (source, target) in enumerate(
            (
                (trailing, following),
                (tables.at[span, pl.ds(size, size)], table.at[pl.ds(size, size)]),
                (recording, hop),
                (tables.at[span, pl.ds(0, size)], table.at[pl.ds(0, size)]),
            )
        )
    ]
    for copy in copies:
        copy.start()
    for copy in copies[:2]:
        copy.wait()
    last = jnp.dot(following[...], table[size:, :], preferred_element_type=jnp.float32)
    for copy in copies[2:]:
        copy.wait()
    for segment, value in enumerate(hop_parts(span, hop[...], table, segments)):
        if segment == segments - 1:
            value += last
        total[:, segment * width : (segment + 1) * width] = value


def finish_kernel(spans, *refs):
    hops, (table, begun, mine, theirs) = refs[: spans - 1], refs[spans - 1 :]
    width = table.shape[1]
    part = width // 2
    low = lax.axis_index("freq") == 0
    parts = [
        hop_parts(lax.rem(lax.axis_index("tm") - step + spans, spans), hop[...], table, spans)
        for step, hop in enumerate(hops, 1)
    ]
    for segment, added in enumerate(zip(*parts)):
        value = begun[:, segment * width : (segment + 1) * width]
        for more in added:
            value += more
        first, second = value[:, :part].astype(jnp.bfloat16), value[:, part:].astype(jnp.bfloat16)
        columns = slice(segment * part, (segment + 1) * part)
        mine[:, columns] = jnp.where(low, first, second)
        theirs[:, columns] = jnp.where(low, second, first)


def block_kernel(own, other, out):
    out[...] = block_of(own, other)


def band_kernel(chain, *refs):
    *weights, out = refs
    blocks, rows, width = out.shape
    here = lax.axis_index("chan")
    low = lax.axis_index("freq") == 0
    for block in range(blocks):
        if chain == 4:
            own, other = (ref[block].astype(jnp.float32) for ref in weights)
            place = jnp.bitwise_xor(here, (0, 1, 3, 2)[block])
            tile = jnp.concatenate([jnp.where(low, own, other), jnp.where(low, other, own)], axis=1).T
        else:
            place = block
            tile = weights[0][block * rows : (block + 1) * rows, :].astype(jnp.float32)
        blank = jnp.zeros((rows, width - tile.shape[1]), jnp.float32)
        wide = jnp.concatenate([tile, blank], axis=1)
        out[place] = pltpu.roll(wide, 0, 1, stride=1, stride_axis=0).astype(jnp.bfloat16)


def whitened(band, window, raw):
    predicted = jnp.dot(band, window, preferred_element_type=jnp.float32)
    return (raw.astype(jnp.float32) - predicted).astype(jnp.bfloat16)


def pair_products(slots, own, spectra_of, segments, scaling, out, left, result, sems):
    rows, columns = own.shape
    left[:rows, :] = own
    half = columns // (2 * segments)
    turned = []
    for segment in range(segments):
        start = 2 * segment * half
        turned += [own[:, start + half : start + 2 * half], -own[:, start : start + half]]
    left[rows:, :] = jnp.concatenate(turned, axis=1)

    contract = (((1,), (1,)), ((), ()))
    for slot in range(SLOTS):
        partner = slots[0, slot]
        theirs = spectra_of(jnp.maximum(partner, 0))
        for part, lhs in enumerate((left[:rows, :], left[rows:, :])):
            value = lax.dot_general(lhs, theirs, contract, preferred_element_type=jnp.float32)
            result[slot, part] = jnp.where(partner >= 0, value * scaling, 0.0)
            pltpu.make_async_copy(result.at[slot, part], out.at[slot, part], sems.at[slot, part]).start()
    for slot in range(SLOTS):
        for part in range(2):
            pltpu.make_async_copy(result.at[slot, part], out.at[slot, part], sems.at[slot, part]).wait()


def cross_kernel(segments, scaling, slots, *refs):
    near = [0] + [d for d in range(-REACH, REACH + 1) if d]
    blocks, (before, after, band, out, padded, spectra, left, result, sems) = refs[: len(near)], refs[len(near) :]
    count, rows, columns = spectra.shape
    rim = before.shape[0]
    edge = count * rows + rim
    padded[:rim, :] = before[...]
    padded[edge : edge + rim, :] = after[...]
    padded[edge + rim :, :] = jnp.zeros((padded.shape[0] - edge - rim, columns), jnp.bfloat16)
    for distance, value in zip(near, blocks):
        start = (distance + REACH) * rows + rim
        padded[start : start + rows, :] = value[...]
    for block in range(count):
        start = block * rows
        window = padded[start : start + band.shape[2], :]
        spectra[block] = whitened(band[block], window, padded[start + rim : start + rim + rows, :])
    base = lax.axis_index("chan") - REACH
    spectra_of = lambda block: spectra[jnp.clip(block - base, 0, count - 1)]
    pair_products(slots, spectra[REACH], spectra_of, segments, scaling, out, left, result, sems)


def chosen(a, b, c, d):
    here = lax.axis_index("chan")
    return jnp.where(here == 0, a, jnp.where(here == 1, b, jnp.where(here == 2, c, d)))


def early_kernel(raw, first, first_other, second, band, padded, spectra):
    count, rows, columns = spectra.shape
    rim = (padded.shape[0] - count * rows) // 4
    edge = count * rows + rim
    padded[:rim, :] = jnp.zeros((rim, columns), jnp.bfloat16)
    padded[edge:, :] = jnp.zeros((3 * rim, columns), jnp.bfloat16)
    last = chosen(3, 2, 1, 0)
    padded[pl.ds(pl.multiple_of(last * rows + rim, rim), rows), :] = jnp.zeros((rows, columns), jnp.bfloat16)
    for place, value in (
        (lax.axis_index("chan"), raw),
        (chosen(1, 3, 0, 2), block_of(first, first_other)),
        (chosen(2, 0, 3, 1), second),
    ):
        padded[pl.ds(pl.multiple_of(place * rows + rim, rim), rows), :] = value[...]
    for block in range(count):
        start = block * rows
        window = padded[start : start + band.shape[2], :]
        spectra[block] = whitened(band[block], window, padded[start + rim : start + rim + rows, :])


def late_kernel(segments, scaling, slots, padded, early, third, fourth, fourth_other, band, out, left, result, sems):
    count, rows, columns = early.shape
    width = band.shape[2]
    rim = (padded.shape[0] - count * rows) // 4
    here = lax.axis_index("chan")
    last = chosen(3, 2, 1, 0)
    inner = (here == 1) | (here == 2)
    value = jnp.where(inner, third[...], block_of(fourth, fourth_other))

    start = pl.multiple_of(last * rows, rows)
    above = padded[pl.ds(start, rim), :]
    below = padded[pl.ds(start + rim + rows, width - rim - rows), :]
    window = jnp.concatenate([above, value, below], axis=0)
    arrived = whitened(band[last], window, value)

    half = rows // 2
    upper = padded[pl.ds(pl.multiple_of(jnp.maximum(start - half, 0), half), half + rim), :]
    window = jnp.concatenate([upper, value[: width - rows - rim]], axis=0)
    bottom = whitened(band[jnp.maximum(last - 1, 0), rows - rim :, half:], window, above)
    lower = below[: LANES - rim]
    window = jnp.concatenate([value[rows - rim :], lower], axis=0)
    top = whitened(band[jnp.minimum(last + 1, count - 1), :rim, :LANES], window, lower[:rim])

    def mended(block, known):
        return jnp.concatenate(
            [
                jnp.where(block == last + 1, top, known[:rim]),
                known[rim : rows - rim],
                jnp.where(block == last - 1, bottom, known[rows - rim :]),
            ],
            axis=0,
        )

    spectra_of = lambda block: mended(block, jnp.where(block == last, arrived, early[block]))
    pair_products(slots, mended(here, early[here]), spectra_of, segments, scaling, out, left, result, sems)


def local(tables, recording, trailing, whiten_filter, pair_list):
    rows, hop = recording.shape
    spans, halves, chain = (lax.axis_size(axis) for axis in ("tm", "freq", "chan"))
    bands = spans * halves
    bins2 = 2 * FB // bands
    block_rows = halves * rows
    taps = whiten_filter.shape[1]
    rim = taps // 2
    here = lax.axis_index("chan")

    in_vmem = pl.BlockSpec(memory_space=pltpu.VMEM)
    small = pltpu.CompilerParams(vmem_limit_bytes=16 * 2**20)

    received = [
        lax.ppermute(recording, "tm", [(i, (i + step) % spans) for i in range(spans)])
        for step in range(1, spans)
    ]
    if chain == 4:
        filters = [
            lax.ppermute(whiten_filter.T, "chan", [(i, i ^ step) for i in range(chain)])
            for step in (1, 3, 2)
        ]
    else:
        filters = [lax.all_gather(whiten_filter, ("chan", "freq"), axis=0, tiled=True)]
    total = (block_rows, spans * bins2)
    in_hbm = pl.BlockSpec(memory_space=pltpu.HBM)
    begun, table = pl.pallas_call(
        begin_kernel,
        out_shape=[
            jax.ShapeDtypeStruct((rows, halves * total[1]), jnp.float32),
            jax.ShapeDtypeStruct(tables.shape[1:], jnp.bfloat16),
        ],
        in_specs=[in_hbm] * 3,
        out_specs=[in_vmem] * 2,
        scratch_shapes=[
            pltpu.VMEM(recording.shape, jnp.bfloat16),
            pltpu.VMEM(trailing.shape, jnp.bfloat16),
            pltpu.SemaphoreType.DMA((4,)),
        ],
        compiler_params=small,
        name="begin_transform",
    )(
        *(
            pltpu.with_memory_space_constraint(value, pltpu.HBM)
            for value in (recording, trailing, jnp.asarray(tables))
        )
    )
    received, filters, begun = lax.optimization_barrier((received, filters, begun))
    half_rows = (rows, total[1])
    mine, theirs = pl.pallas_call(
        functools.partial(finish_kernel, spans),
        out_shape=[jax.ShapeDtypeStruct(half_rows, jnp.bfloat16)] * 2,
        in_specs=[in_vmem] * (spans + 1),
        out_specs=[in_vmem] * 2,
        compiler_params=small,
        name="finish_transform",
    )(*received, table, begun)
    raw = pl.pallas_call(
        block_kernel,
        out_shape=jax.ShapeDtypeStruct(total, jnp.bfloat16),
        in_specs=[in_vmem] * 2,
        out_specs=in_vmem,
        compiler_params=small,
        name="block",
    )(mine, swapped(theirs, "freq"))

    if chain == 4:
        near = chain
        weights = jnp.stack([whiten_filter.T, *filters])
        weights = (weights, swapped(weights, "freq"))
    else:
        near = 2 * REACH + 1
        beyond = jnp.pad(filters[0], ((REACH * block_rows, REACH * block_rows), (0, 0)))
        weights = (lax.dynamic_slice_in_dim(beyond, here * block_rows, near * block_rows, 0),)
    window = -(-(block_rows + taps) // LANES) * LANES
    band = pl.pallas_call(
        functools.partial(band_kernel, chain),
        out_shape=jax.ShapeDtypeStruct((near, block_rows, window), jnp.bfloat16),
        in_specs=[in_vmem] * len(weights),
        out_specs=in_vmem,
        compiler_params=small,
        name="band_matrix",
    )(*weights)

    if chain == 4:
        route = [(0, 2), (2, 3), (3, 1), (1, 0)]
        first = lax.ppermute(mine, "chan", route)
        across = [(2 * i + half, 2 * j + 1 - half) for i, j in route for half in range(2)]
        first_other = lax.ppermute(theirs, ("chan", "freq"), across)
        second = lax.ppermute(raw, "chan", [(1, 3), (3, 2), (2, 0), (0, 1)])
        third = lax.ppermute(raw, "chan", [(1, 2), (2, 1)])
        last = [lax.ppermute(value, "chan", [(1, 0), (2, 3)]) for value in (first, first_other)]
    else:

        def shifted(value, distance):
            route = [(i - distance, i) for i in range(chain) if 0 <= i - distance < chain]
            return lax.ppermute(value, "chan", route)

        blocks = [raw]
        blocks += [shifted(raw, -d) for d in range(-REACH, REACH + 1) if d]
        blocks.append(shifted(raw[block_rows - rim :, :], REACH + 1))
        blocks.append(shifted(raw[:rim, :], -REACH - 1))

    padded = (near * block_rows + 4 * rim, total[1])
    spectra = (near, *total)
    if chain == 4:
        operands = pl.pallas_call(
            early_kernel,
            out_shape=[jax.ShapeDtypeStruct(shape, jnp.bfloat16) for shape in (padded, spectra)],
            in_specs=[in_vmem] * 5,
            out_specs=[in_vmem] * 2,
            compiler_params=small,
            name="early_whitening",
        )(raw, first, first_other, second, band)
        operands = (*operands, third, *last, band)
        kernel, scratch = late_kernel, []
    else:
        operands = (*blocks, band)
        kernel, scratch = cross_kernel, [pltpu.VMEM(shape, jnp.bfloat16) for shape in (padded, spectra)]
    out_shape = (SLOTS, 2, block_rows, block_rows)
    result = pl.pallas_call(
        functools.partial(kernel, spans, 1.0 / math.sqrt(spans * bins2 // 2)),
        out_shape=jax.ShapeDtypeStruct(out_shape, jnp.float32),
        in_specs=[pl.BlockSpec(memory_space=pltpu.SMEM)] + [in_vmem] * len(operands),
        out_specs=in_hbm,
        scratch_shapes=[
            *scratch,
            pltpu.VMEM((2 * block_rows, total[1]), jnp.bfloat16),
            pltpu.VMEM(out_shape, jnp.float32),
            pltpu.SemaphoreType.DMA((SLOTS, 2)),
        ],
        compiler_params=pltpu.CompilerParams(vmem_limit_bytes=24 * 2**20),
        name="cross",
    )(pair_list, *operands)
    return result.reshape(1, SLOTS, 1, 2, block_rows, block_rows)


def solution(mesh):
    placed = (
        P(("days", "chan", "freq"), "tm"),
        P(("days", "chan", "freq"), None),
        P(("chan", "freq"), None),
        P(("days", "chan"), None),
    )

    def step(recording, trailing, whiten_filter, pair_list):
        tables = band_tables(mesh.shape["tm"], mesh.shape["freq"], 2 * trailing.shape[1])
        return jax.shard_map(
            functools.partial(local, tables),
            mesh=mesh,
            in_specs=placed,
            out_specs=P(("days", "chan"), None, ("tm", "freq"), None, None, None),
            check_vma=False,
        )(recording, trailing, whiten_filter, pair_list)

    return step
```

```python
import functools
import math

import jax
import jax.numpy as jnp
import ml_dtypes
import numpy as np
from jax import lax
from jax.experimental import pallas as pl
from jax.experimental.pallas import tpu as pltpu
from jax.sharding import PartitionSpec as P

FB = 512
REACH = 3
SLOTS = 4
LANES = 128


def band_tables(spans, halves, length):
    samples = np.arange(length, dtype=np.int64)[:, None]
    bins = np.arange(FB, dtype=np.int64)[None, :]
    phase = (samples * bins % length).astype(np.float32)
    angle = np.float32(2.0 * math.pi / length) * phase
    ramp = np.float32(2.0 * math.pi / length) * np.arange(length, dtype=np.float32)
    taper = (np.float32(0.5) - np.float32(0.5) * np.cos(ramp))[:, None]
    normaliser = np.float32(1.0 / math.sqrt(0.375 * length))
    cosine = (taper * np.cos(angle) * normaliser).astype(ml_dtypes.bfloat16)
    sine = (-taper * np.sin(angle) * normaliser).astype(ml_dtypes.bfloat16)
    both = np.stack([cosine, sine], axis=1).reshape(length, 2, spans, halves, -1)
    return np.ascontiguousarray(both.transpose(2, 0, 3, 1, 4)).reshape(spans, length, -1)


def swapped(value, axis):
    return lax.ppermute(value, axis, [(0, 1), (1, 0)])


def block_of(own, other):
    low = lax.axis_index("freq") == 0
    a, b = own[...], other[...]
    return jnp.concatenate([jnp.where(low, a, b), jnp.where(low, b, a)], axis=0)


def hop_parts(place, value, table, segments):
    hop = value.shape[1]
    first = jnp.dot(value, table[:hop, :], preferred_element_type=jnp.float32)
    second = jnp.dot(value, table[hop:, :], preferred_element_type=jnp.float32)
    for segment in range(segments):
        yield jnp.where(place == segment, first, jnp.where(place == segment + 1, second, 0.0))


def begin_kernel(recording, trailing, tables, total, table, hop, following, sems):
    span = lax.axis_index("tm")
    width = table.shape[1]
    segments = total.shape[1] // width
    size = hop.shape[1]
    copies = [
        pltpu.make_async_copy(source, target, sems.at[index])
        for index, (source, target) in enumerate(
            (
                (trailing, following),
                (tables.at[span, pl.ds(size, size)], table.at[pl.ds(size, size)]),
                (recording, hop),
                (tables.at[span, pl.ds(0, size)], table.at[pl.ds(0, size)]),
            )
        )
    ]
    for copy in copies:
        copy.start()
    for copy in copies[:2]:
        copy.wait()
    last = jnp.dot(following[...], table[size:, :], preferred_element_type=jnp.float32)
    for copy in copies[2:]:
        copy.wait()
    for segment, value in enumerate(hop_parts(span, hop[...], table, segments)):
        if segment == segments - 1:
            value += last
        total[:, segment * width : (segment + 1) * width] = value


def finish_kernel(spans, *refs):
    hops, (table, begun, mine, theirs, both) = refs[: spans - 1], refs[spans - 1 :]
    rows = mine.shape[0]
    width = table.shape[1]
    part = width // 2
    low = lax.axis_index("freq") == 0
    parts = [
        hop_parts(lax.rem(lax.axis_index("tm") - step + spans, spans), hop[...], table, spans)
        for step, hop in enumerate(hops, 1)
    ]
    for segment, added in enumerate(zip(*parts)):
        value = begun[:, segment * width : (segment + 1) * width]
        for more in added:
            value += more
        first, second = value[:, :part].astype(jnp.bfloat16), value[:, part:].astype(jnp.bfloat16)
        columns = slice(segment * part, (segment + 1) * part)
        mine[:, columns] = both[:rows, columns] = jnp.where(low, first, second)
        theirs[:, columns] = both[rows:, columns] = jnp.where(low, second, first)


def block_kernel(own, other, out):
    out[...] = block_of(own, other)


def lower_kernel(value, out):
    out[...] = value[out.shape[0] :, :]


def band_kernel(chain, *refs):
    *weights, out = refs
    blocks, rows, width = out.shape
    here = lax.axis_index("chan")
    low = lax.axis_index("freq") == 0
    for block in range(blocks):
        if chain == 4:
            own, other = (ref[block].astype(jnp.float32) for ref in weights)
            place = jnp.bitwise_xor(here, (0, 1, 3, 2)[block])
            tile = jnp.concatenate([jnp.where(low, own, other), jnp.where(low, other, own)], axis=1).T
        else:
            place = block
            tile = weights[0][block * rows : (block + 1) * rows, :].astype(jnp.float32)
        blank = jnp.zeros((rows, width - tile.shape[1]), jnp.float32)
        wide = jnp.concatenate([tile, blank], axis=1)
        out[place] = pltpu.roll(wide, 0, 1, stride=1, stride_axis=0).astype(jnp.bfloat16)


def whitened(band, window, raw):
    predicted = jnp.dot(band, window, preferred_element_type=jnp.float32)
    return (raw.astype(jnp.float32) - predicted).astype(jnp.bfloat16)


def pair_products(slots, own, spectra_of, segments, scaling, out, left, result, sems):
    rows, columns = own.shape
    left[:rows, :] = own
    half = columns // (2 * segments)
    turned = []
    for segment in range(segments):
        start = 2 * segment * half
        turned += [own[:, start + half : start + 2 * half], -own[:, start : start + half]]
    left[rows:, :] = jnp.concatenate(turned, axis=1)

    contract = (((1,), (1,)), ((), ()))
    for slot in range(SLOTS):
        partner = slots[0, slot]
        theirs = spectra_of(jnp.maximum(partner, 0))
        for part, lhs in enumerate((left[:rows, :], left[rows:, :])):
            value = lax.dot_general(lhs, theirs, contract, preferred_element_type=jnp.float32)
            result[slot, part] = jnp.where(partner >= 0, value * scaling, 0.0)
            pltpu.make_async_copy(result.at[slot, part], out.at[slot, part], sems.at[slot, part]).start()
    for slot in range(SLOTS):
        for part in range(2):
            pltpu.make_async_copy(result.at[slot, part], out.at[slot, part], sems.at[slot, part]).wait()


def cross_kernel(segments, scaling, slots, *refs):
    near = [0] + [d for d in range(-REACH, REACH + 1) if d]
    blocks, (before, after, band, out, padded, spectra, left, result, sems) = refs[: len(near)], refs[len(near) :]
    count, rows, columns = spectra.shape
    rim = before.shape[0]
    edge = count * rows + rim
    padded[:rim, :] = before[...]
    padded[edge : edge + rim, :] = after[...]
    padded[edge + rim :, :] = jnp.zeros((padded.shape[0] - edge - rim, columns), jnp.bfloat16)
    for distance, value in zip(near, blocks):
        start = (distance + REACH) * rows + rim
        padded[start : start + rows, :] = value[...]
    for block in range(count):
        start = block * rows
        window = padded[start : start + band.shape[2], :]
        spectra[block] = whitened(band[block], window, padded[start + rim : start + rim + rows, :])
    base = lax.axis_index("chan") - REACH
    spectra_of = lambda block: spectra[jnp.clip(block - base, 0, count - 1)]
    pair_products(slots, spectra[REACH], spectra_of, segments, scaling, out, left, result, sems)


def chosen(a, b, c, d):
    here = lax.axis_index("chan")
    return jnp.where(here == 0, a, jnp.where(here == 1, b, jnp.where(here == 2, c, d)))


def early_kernel(raw, first, first_other, second, second_other, band, padded, spectra):
    count, rows, columns = spectra.shape
    rim = (padded.shape[0] - count * rows) // 4
    edge = count * rows + rim
    padded[:rim, :] = jnp.zeros((rim, columns), jnp.bfloat16)
    padded[edge:, :] = jnp.zeros((3 * rim, columns), jnp.bfloat16)
    last = chosen(3, 2, 1, 0)
    padded[pl.ds(pl.multiple_of(last * rows + rim, rim), rows), :] = jnp.zeros((rows, columns), jnp.bfloat16)
    for place, value in (
        (lax.axis_index("chan"), raw),
        (chosen(1, 3, 0, 2), block_of(first, first_other)),
        (chosen(2, 0, 3, 1), block_of(second[: second_other.shape[0], :], second_other)),
    ):
        padded[pl.ds(pl.multiple_of(place * rows + rim, rim), rows), :] = value[...]
    for block in range(count):
        start = block * rows
        window = padded[start : start + band.shape[2], :]
        spectra[block] = whitened(band[block], window, padded[start + rim : start + rim + rows, :])


def late_kernel(segments, scaling, slots, padded, early, third, fourth, fourth_other, band, out, left, result, sems):
    count, rows, columns = early.shape
    width = band.shape[2]
    rim = (padded.shape[0] - count * rows) // 4
    here = lax.axis_index("chan")
    last = chosen(3, 2, 1, 0)
    inner = (here == 1) | (here == 2)
    value = jnp.where(inner, third[...], block_of(fourth, fourth_other))

    start = pl.multiple_of(last * rows, rows)
    above = padded[pl.ds(start, rim), :]
    below = padded[pl.ds(start + rim + rows, width - rim - rows), :]
    window = jnp.concatenate([above, value, below], axis=0)
    arrived = whitened(band[last], window, value)

    half = rows // 2
    upper = padded[pl.ds(pl.multiple_of(jnp.maximum(start - half, 0), half), half + rim), :]
    window = jnp.concatenate([upper, value[: width - rows - rim]], axis=0)
    bottom = whitened(band[jnp.maximum(last - 1, 0), rows - rim :, half:], window, above)
    lower = below[: LANES - rim]
    window = jnp.concatenate([value[rows - rim :], lower], axis=0)
    top = whitened(band[jnp.minimum(last + 1, count - 1), :rim, :LANES], window, lower[:rim])

    def mended(block, known):
        return jnp.concatenate(
            [
                jnp.where(block == last + 1, top, known[:rim]),
                known[rim : rows - rim],
                jnp.where(block == last - 1, bottom, known[rows - rim :]),
            ],
            axis=0,
        )

    spectra_of = lambda block: mended(block, jnp.where(block == last, arrived, early[block]))
    pair_products(slots, mended(here, early[here]), spectra_of, segments, scaling, out, left, result, sems)


def local(tables, recording, trailing, whiten_filter, pair_list):
    rows, hop = recording.shape
    spans, halves, chain = (lax.axis_size(axis) for axis in ("tm", "freq", "chan"))
    bands = spans * halves
    bins2 = 2 * FB // bands
    block_rows = halves * rows
    taps = whiten_filter.shape[1]
    rim = taps // 2
    here = lax.axis_index("chan")

    in_vmem = pl.BlockSpec(memory_space=pltpu.VMEM)
    small = pltpu.CompilerParams(vmem_limit_bytes=16 * 2**20)

    received = [
        lax.ppermute(recording, "tm", [(i, (i + step) % spans) for i in range(spans)])
        for step in range(1, spans)
    ]
    if chain == 4:
        filters = [
            lax.ppermute(whiten_filter.T, "chan", [(i, i ^ step) for i in range(chain)])
            for step in (1, 3, 2)
        ]
    else:
        filters = [lax.all_gather(whiten_filter, ("chan", "freq"), axis=0, tiled=True)]
    total = (block_rows, spans * bins2)
    in_hbm = pl.BlockSpec(memory_space=pltpu.HBM)
    begun, table = pl.pallas_call(
        begin_kernel,
        out_shape=[
            jax.ShapeDtypeStruct((rows, halves * total[1]), jnp.float32),
            jax.ShapeDtypeStruct(tables.shape[1:], jnp.bfloat16),
        ],
        in_specs=[in_hbm] * 3,
        out_specs=[in_vmem] * 2,
        scratch_shapes=[
            pltpu.VMEM(recording.shape, jnp.bfloat16),
            pltpu.VMEM(trailing.shape, jnp.bfloat16),
            pltpu.SemaphoreType.DMA((4,)),
        ],
        compiler_params=small,
        name="begin_transform",
    )(
        *(
            pltpu.with_memory_space_constraint(value, pltpu.HBM)
            for value in (recording, trailing, jnp.asarray(tables))
        )
    )
    received, filters, begun = lax.optimization_barrier((received, filters, begun))
    half_rows = (rows, total[1])
    mine, theirs, both = pl.pallas_call(
        functools.partial(finish_kernel, spans),
        out_shape=[jax.ShapeDtypeStruct(shape, jnp.bfloat16) for shape in (half_rows, half_rows, total)],
        in_specs=[in_vmem] * (spans + 1),
        out_specs=[in_vmem] * 3,
        compiler_params=small,
        name="finish_transform",
    )(*received, table, begun)
    raw = pl.pallas_call(
        block_kernel,
        out_shape=jax.ShapeDtypeStruct(total, jnp.bfloat16),
        in_specs=[in_vmem] * 2,
        out_specs=in_vmem,
        compiler_params=small,
        name="block",
    )(mine, swapped(theirs, "freq"))

    if chain == 4:
        near = chain
        weights = jnp.stack([whiten_filter.T, *filters])
        weights = (weights, swapped(weights, "freq"))
    else:
        near = 2 * REACH + 1
        beyond = jnp.pad(filters[0], ((REACH * block_rows, REACH * block_rows), (0, 0)))
        weights = (lax.dynamic_slice_in_dim(beyond, here * block_rows, near * block_rows, 0),)
    window = -(-(block_rows + taps) // LANES) * LANES
    band = pl.pallas_call(
        functools.partial(band_kernel, chain),
        out_shape=jax.ShapeDtypeStruct((near, block_rows, window), jnp.bfloat16),
        in_specs=[in_vmem] * len(weights),
        out_specs=in_vmem,
        compiler_params=small,
        name="band_matrix",
    )(*weights)

    if chain == 4:
        route = [(0, 2), (2, 3), (3, 1), (1, 0)]
        first = lax.ppermute(mine, "chan", route)
        across = [(2 * i + half, 2 * j + 1 - half) for i, j in route for half in range(2)]
        first_other = lax.ppermute(theirs, ("chan", "freq"), across)
        second = lax.ppermute(both, "chan", [(1, 3), (3, 2), (2, 0), (0, 1)])
        lower = pl.pallas_call(
            lower_kernel,
            out_shape=jax.ShapeDtypeStruct(half_rows, jnp.bfloat16),
            in_specs=[in_vmem],
            out_specs=in_vmem,
            compiler_params=small,
            name="lower_rows",
        )(second)
        second_other = swapped(lower, "freq")
        third = lax.ppermute(raw, "chan", [(1, 2), (2, 1)])
        last = [lax.ppermute(value, "chan", [(1, 0), (2, 3)]) for value in (first, first_other)]
    else:

        def shifted(value, distance):
            route = [(i - distance, i) for i in range(chain) if 0 <= i - distance < chain]
            return lax.ppermute(value, "chan", route)

        blocks = [raw]
        blocks += [shifted(raw, -d) for d in range(-REACH, REACH + 1) if d]
        blocks.append(shifted(raw[block_rows - rim :, :], REACH + 1))
        blocks.append(shifted(raw[:rim, :], -REACH - 1))

    padded = (near * block_rows + 4 * rim, total[1])
    spectra = (near, *total)
    if chain == 4:
        operands = pl.pallas_call(
            early_kernel,
            out_shape=[jax.ShapeDtypeStruct(shape, jnp.bfloat16) for shape in (padded, spectra)],
            in_specs=[in_vmem] * 6,
            out_specs=[in_vmem] * 2,
            compiler_params=small,
            name="early_whitening",
        )(raw, first, first_other, second, second_other, band)
        operands = (*operands, third, *last, band)
        kernel, scratch = late_kernel, []
    else:
        operands = (*blocks, band)
        kernel, scratch = cross_kernel, [pltpu.VMEM(shape, jnp.bfloat16) for shape in (padded, spectra)]
    out_shape = (SLOTS, 2, block_rows, block_rows)
    result = pl.pallas_call(
        functools.partial(kernel, spans, 1.0 / math.sqrt(spans * bins2 // 2)),
        out_shape=jax.ShapeDtypeStruct(out_shape, jnp.float32),
        in_specs=[pl.BlockSpec(memory_space=pltpu.SMEM)] + [in_vmem] * len(operands),
        out_specs=in_hbm,
        scratch_shapes=[
            *scratch,
            pltpu.VMEM((2 * block_rows, total[1]), jnp.bfloat16),
            pltpu.VMEM(out_shape, jnp.float32),
            pltpu.SemaphoreType.DMA((SLOTS, 2)),
        ],
        compiler_params=pltpu.CompilerParams(vmem_limit_bytes=24 * 2**20),
        name="cross",
    )(pair_list, *operands)
    return result.reshape(1, SLOTS, 1, 2, block_rows, block_rows)


def solution(mesh):
    placed = (
        P(("days", "chan", "freq"), "tm"),
        P(("days", "chan", "freq"), None),
        P(("chan", "freq"), None),
        P(("days", "chan"), None),
    )

    def step(recording, trailing, whiten_filter, pair_list):
        tables = band_tables(mesh.shape["tm"], mesh.shape["freq"], 2 * trailing.shape[1])
        return jax.shard_map(
            functools.partial(local, tables),
            mesh=mesh,
            in_specs=placed,
            out_specs=P(("days", "chan"), None, ("tm", "freq"), None, None, None),
            check_vma=False,
        )(recording, trailing, whiten_filter, pair_list)

    return step
```

```python
import functools
import math

import jax
import jax.numpy as jnp
import ml_dtypes
import numpy as np
from jax import lax
from jax.experimental import pallas as pl
from jax.experimental.pallas import tpu as pltpu
from jax.sharding import PartitionSpec as P

FB = 512
REACH = 3
SLOTS = 4
LANES = 128


def band_tables(spans, halves, length):
    samples = np.arange(length, dtype=np.int64)[:, None]
    bins = np.arange(FB, dtype=np.int64)[None, :]
    phase = (samples * bins % length).astype(np.float32)
    angle = np.float32(2.0 * math.pi / length) * phase
    ramp = np.float32(2.0 * math.pi / length) * np.arange(length, dtype=np.float32)
    taper = (np.float32(0.5) - np.float32(0.5) * np.cos(ramp))[:, None]
    normaliser = np.float32(1.0 / math.sqrt(0.375 * length))
    cosine = (taper * np.cos(angle) * normaliser).astype(ml_dtypes.bfloat16)
    sine = (-taper * np.sin(angle) * normaliser).astype(ml_dtypes.bfloat16)
    both = np.stack([cosine, sine], axis=1).reshape(length, 2, spans, halves, -1)
    return np.ascontiguousarray(both.transpose(2, 0, 3, 1, 4)).reshape(spans, length, -1)


def swapped(value, axis):
    return lax.ppermute(value, axis, [(0, 1), (1, 0)])


def block_of(own, other):
    low = lax.axis_index("freq") == 0
    a, b = own[...], other[...]
    return jnp.concatenate([jnp.where(low, a, b), jnp.where(low, b, a)], axis=0)


def hop_parts(place, value, table, segments):
    hop = value.shape[1]
    first = jnp.dot(value, table[:hop, :], preferred_element_type=jnp.float32)
    second = jnp.dot(value, table[hop:, :], preferred_element_type=jnp.float32)
    for segment in range(segments):
        yield jnp.where(place == segment, first, jnp.where(place == segment + 1, second, 0.0))


def begin_kernel(recording, trailing, tables, total, table, hop, following, sems):
    span = lax.axis_index("tm")
    width = table.shape[1]
    segments = total.shape[1] // width
    size = hop.shape[1]
    copies = [
        pltpu.make_async_copy(source, target, sems.at[index])
        for index, (source, target) in enumerate(
            (
                (trailing, following),
                (tables.at[span, pl.ds(size, size)], table.at[pl.ds(size, size)]),
                (recording, hop),
                (tables.at[span, pl.ds(0, size)], table.at[pl.ds(0, size)]),
            )
        )
    ]
    for copy in copies:
        copy.start()
    for copy in copies[:2]:
        copy.wait()
    last = jnp.dot(following[...], table[size:, :], preferred_element_type=jnp.float32)
    for copy in copies[2:]:
        copy.wait()
    for segment, value in enumerate(hop_parts(span, hop[...], table, segments)):
        if segment == segments - 1:
            value += last
        total[:, segment * width : (segment + 1) * width] = value


def finish_kernel(spans, *refs):
    hops, (table, begun, mine, theirs, both) = refs[: spans - 1], refs[spans - 1 :]
    rows = mine.shape[0]
    width = table.shape[1]
    part = width // 2
    low = lax.axis_index("freq") == 0
    parts = [
        hop_parts(lax.rem(lax.axis_index("tm") - step + spans, spans), hop[...], table, spans)
        for step, hop in enumerate(hops, 1)
    ]
    for segment, added in enumerate(zip(*parts)):
        value = begun[:, segment * width : (segment + 1) * width]
        for more in added:
            value += more
        first, second = value[:, :part].astype(jnp.bfloat16), value[:, part:].astype(jnp.bfloat16)
        columns = slice(segment * part, (segment + 1) * part)
        mine[:, columns] = both[:rows, columns] = jnp.where(low, first, second)
        theirs[:, columns] = both[rows:, columns] = jnp.where(low, second, first)


def block_kernel(own, other, out):
    out[...] = block_of(own, other)


def lower_kernel(value, out):
    out[...] = value[out.shape[0] :, :]


def band_kernel(chain, *refs):
    *weights, out = refs
    blocks, rows, width = out.shape
    here = lax.axis_index("chan")
    low = lax.axis_index("freq") == 0
    for block in range(blocks):
        if chain == 4:
            own, other = (ref[block].astype(jnp.float32) for ref in weights)
            place = jnp.bitwise_xor(here, (0, 1, 3, 2)[block])
            tile = jnp.concatenate([jnp.where(low, own, other), jnp.where(low, other, own)], axis=1).T
        else:
            place = block
            tile = weights[0][block * rows : (block + 1) * rows, :].astype(jnp.float32)
        blank = jnp.zeros((rows, width - tile.shape[1]), jnp.float32)
        wide = jnp.concatenate([tile, blank], axis=1)
        out[place] = pltpu.roll(wide, 0, 1, stride=1, stride_axis=0).astype(jnp.bfloat16)


def whitened(band, window, raw):
    predicted = jnp.dot(band, window, preferred_element_type=jnp.float32)
    return (raw.astype(jnp.float32) - predicted).astype(jnp.bfloat16)


def pair_products(slots, own, spectra_of, segments, scaling, out, left, result, sems):
    rows, columns = own.shape
    left[:rows, :] = own
    half = columns // (2 * segments)
    turned = []
    for segment in range(segments):
        start = 2 * segment * half
        turned += [own[:, start + half : start + 2 * half], -own[:, start : start + half]]
    left[rows:, :] = jnp.concatenate(turned, axis=1)

    contract = (((1,), (1,)), ((), ()))
    for slot in range(SLOTS):
        partner = slots[0, slot]
        theirs = spectra_of(jnp.maximum(partner, 0))
        for part, lhs in enumerate((left[:rows, :], left[rows:, :])):
            value = lax.dot_general(lhs, theirs, contract, preferred_element_type=jnp.float32)
            result[slot, part] = jnp.where(partner >= 0, value * scaling, 0.0)
            pltpu.make_async_copy(result.at[slot, part], out.at[slot, part], sems.at[slot, part]).start()
    for slot in range(SLOTS):
        for part in range(2):
            pltpu.make_async_copy(result.at[slot, part], out.at[slot, part], sems.at[slot, part]).wait()


def cross_kernel(segments, scaling, slots, *refs):
    near = [0] + [d for d in range(-REACH, REACH + 1) if d]
    blocks, (before, after, band, out, padded, spectra, left, result, sems) = refs[: len(near)], refs[len(near) :]
    count, rows, columns = spectra.shape
    rim = before.shape[0]
    edge = count * rows + rim
    padded[:rim, :] = before[...]
    padded[edge : edge + rim, :] = after[...]
    padded[edge + rim :, :] = jnp.zeros((padded.shape[0] - edge - rim, columns), jnp.bfloat16)
    for distance, value in zip(near, blocks):
        start = (distance + REACH) * rows + rim
        padded[start : start + rows, :] = value[...]
    for block in range(count):
        start = block * rows
        window = padded[start : start + band.shape[2], :]
        spectra[block] = whitened(band[block], window, padded[start + rim : start + rim + rows, :])
    base = lax.axis_index("chan") - REACH
    spectra_of = lambda block: spectra[jnp.clip(block - base, 0, count - 1)]
    pair_products(slots, spectra[REACH], spectra_of, segments, scaling, out, left, result, sems)


def chosen(a, b, c, d):
    here = lax.axis_index("chan")
    return jnp.where(here == 0, a, jnp.where(here == 1, b, jnp.where(here == 2, c, d)))


def early_kernel(raw, first, first_other, second, second_other, band, padded, spectra, beside, middle):
    count, rows, columns = spectra.shape
    rim = (padded.shape[0] - count * rows) // 4
    edge = count * rows + rim
    padded[:rim, :] = jnp.zeros((rim, columns), jnp.bfloat16)
    padded[edge:, :] = jnp.zeros((3 * rim, columns), jnp.bfloat16)
    last = chosen(3, 2, 1, 0)
    padded[pl.ds(pl.multiple_of(last * rows + rim, rim), rows), :] = jnp.zeros((rows, columns), jnp.bfloat16)
    for place, value in (
        (lax.axis_index("chan"), raw),
        (chosen(1, 3, 0, 2), block_of(first, first_other)),
        (chosen(2, 0, 3, 1), block_of(second[: second_other.shape[0], :], second_other)),
    ):
        padded[pl.ds(pl.multiple_of(place * rows + rim, rim), rows), :] = value[...]
    for block in range(count):
        start = block * rows
        window = padded[start : start + band.shape[2], :]
        spectra[block] = whitened(band[block], window, padded[start + rim : start + rim + rows, :])

    window = padded[pl.ds(pl.multiple_of(last * rows, rows), band.shape[2]), :]
    beside[...] = jnp.dot(band[last], window, preferred_element_type=jnp.float32)
    wide = band[last].astype(jnp.float32)
    middle[...] = pltpu.roll(wide, band.shape[2] - rim, 1)[:, :rows].astype(jnp.bfloat16)


def late_kernel(segments, scaling, slots, padded, early, beside, middle, third, fourth, fourth_other, band, out, left, result, sems):
    count, rows, columns = early.shape
    width = band.shape[2]
    rim = (padded.shape[0] - count * rows) // 4
    here = lax.axis_index("chan")
    last = chosen(3, 2, 1, 0)
    inner = (here == 1) | (here == 2)
    value = jnp.where(inner, third[...], block_of(fourth, fourth_other))

    start = pl.multiple_of(last * rows, rows)
    above = padded[pl.ds(start, rim), :]
    below = padded[pl.ds(start + rim + rows, width - rim - rows), :]
    predicted = jnp.dot(middle[...], value, preferred_element_type=jnp.float32) + beside[...]
    arrived = (value.astype(jnp.float32) - predicted).astype(jnp.bfloat16)

    half = rows // 2
    upper = padded[pl.ds(pl.multiple_of(jnp.maximum(start - half, 0), half), half + rim), :]
    window = jnp.concatenate([upper, value[: width - rows - rim]], axis=0)
    bottom = whitened(band[jnp.maximum(last - 1, 0), rows - rim :, half:], window, above)
    lower = below[: LANES - rim]
    window = jnp.concatenate([value[rows - rim :], lower], axis=0)
    top = whitened(band[jnp.minimum(last + 1, count - 1), :rim, :LANES], window, lower[:rim])

    def mended(block, known):
        return jnp.concatenate(
            [
                jnp.where(block == last + 1, top, known[:rim]),
                known[rim : rows - rim],
                jnp.where(block == last - 1, bottom, known[rows - rim :]),
            ],
            axis=0,
        )

    spectra_of = lambda block: mended(block, jnp.where(block == last, arrived, early[block]))
    pair_products(slots, mended(here, early[here]), spectra_of, segments, scaling, out, left, result, sems)


def local(tables, recording, trailing, whiten_filter, pair_list):
    rows, hop = recording.shape
    spans, halves, chain = (lax.axis_size(axis) for axis in ("tm", "freq", "chan"))
    bands = spans * halves
    bins2 = 2 * FB // bands
    block_rows = halves * rows
    taps = whiten_filter.shape[1]
    rim = taps // 2
    here = lax.axis_index("chan")

    in_vmem = pl.BlockSpec(memory_space=pltpu.VMEM)
    small = pltpu.CompilerParams(vmem_limit_bytes=16 * 2**20)

    received = [
        lax.ppermute(recording, "tm", [(i, (i + step) % spans) for i in range(spans)])
        for step in range(1, spans)
    ]
    if chain == 4:
        filters = [
            lax.ppermute(whiten_filter.T, "chan", [(i, i ^ step) for i in range(chain)])
            for step in (1, 3, 2)
        ]
    else:
        filters = [lax.all_gather(whiten_filter, ("chan", "freq"), axis=0, tiled=True)]
    total = (block_rows, spans * bins2)
    in_hbm = pl.BlockSpec(memory_space=pltpu.HBM)
    begun, table = pl.pallas_call(
        begin_kernel,
        out_shape=[
            jax.ShapeDtypeStruct((rows, halves * total[1]), jnp.float32),
            jax.ShapeDtypeStruct(tables.shape[1:], jnp.bfloat16),
        ],
        in_specs=[in_hbm] * 3,
        out_specs=[in_vmem] * 2,
        scratch_shapes=[
            pltpu.VMEM(recording.shape, jnp.bfloat16),
            pltpu.VMEM(trailing.shape, jnp.bfloat16),
            pltpu.SemaphoreType.DMA((4,)),
        ],
        compiler_params=small,
        name="begin_transform",
    )(
        *(
            pltpu.with_memory_space_constraint(value, pltpu.HBM)
            for value in (recording, trailing, jnp.asarray(tables))
        )
    )
    received, filters, begun = lax.optimization_barrier((received, filters, begun))
    half_rows = (rows, total[1])
    mine, theirs, both = pl.pallas_call(
        functools.partial(finish_kernel, spans),
        out_shape=[jax.ShapeDtypeStruct(shape, jnp.bfloat16) for shape in (half_rows, half_rows, total)],
        in_specs=[in_vmem] * (spans + 1),
        out_specs=[in_vmem] * 3,
        compiler_params=small,
        name="finish_transform",
    )(*received, table, begun)
    raw = pl.pallas_call(
        block_kernel,
        out_shape=jax.ShapeDtypeStruct(total, jnp.bfloat16),
        in_specs=[in_vmem] * 2,
        out_specs=in_vmem,
        compiler_params=small,
        name="block",
    )(mine, swapped(theirs, "freq"))

    if chain == 4:
        near = chain
        weights = jnp.stack([whiten_filter.T, *filters])
        weights = (weights, swapped(weights, "freq"))
    else:
        near = 2 * REACH + 1
        beyond = jnp.pad(filters[0], ((REACH * block_rows, REACH * block_rows), (0, 0)))
        weights = (lax.dynamic_slice_in_dim(beyond, here * block_rows, near * block_rows, 0),)
    window = -(-(block_rows + taps) // LANES) * LANES
    band = pl.pallas_call(
        functools.partial(band_kernel, chain),
        out_shape=jax.ShapeDtypeStruct((near, block_rows, window), jnp.bfloat16),
        in_specs=[in_vmem] * len(weights),
        out_specs=in_vmem,
        compiler_params=small,
        name="band_matrix",
    )(*weights)

    if chain == 4:
        route = [(0, 2), (2, 3), (3, 1), (1, 0)]
        first = lax.ppermute(mine, "chan", route)
        across = [(2 * i + half, 2 * j + 1 - half) for i, j in route for half in range(2)]
        first_other = lax.ppermute(theirs, ("chan", "freq"), across)
        second = lax.ppermute(both, "chan", [(1, 3), (3, 2), (2, 0), (0, 1)])
        lower = pl.pallas_call(
            lower_kernel,
            out_shape=jax.ShapeDtypeStruct(half_rows, jnp.bfloat16),
            in_specs=[in_vmem],
            out_specs=in_vmem,
            compiler_params=small,
            name="lower_rows",
        )(second)
        second_other = swapped(lower, "freq")
        third = lax.ppermute(raw, "chan", [(1, 2), (2, 1)])
        last = [lax.ppermute(value, "chan", [(1, 0), (2, 3)]) for value in (first, first_other)]
    else:

        def shifted(value, distance):
            route = [(i - distance, i) for i in range(chain) if 0 <= i - distance < chain]
            return lax.ppermute(value, "chan", route)

        blocks = [raw]
        blocks += [shifted(raw, -d) for d in range(-REACH, REACH + 1) if d]
        blocks.append(shifted(raw[block_rows - rim :, :], REACH + 1))
        blocks.append(shifted(raw[:rim, :], -REACH - 1))

    padded = (near * block_rows + 4 * rim, total[1])
    spectra = (near, *total)
    if chain == 4:
        operands = pl.pallas_call(
            early_kernel,
            out_shape=[
                jax.ShapeDtypeStruct(padded, jnp.bfloat16),
                jax.ShapeDtypeStruct(spectra, jnp.bfloat16),
                jax.ShapeDtypeStruct(total, jnp.float32),
                jax.ShapeDtypeStruct((block_rows, block_rows), jnp.bfloat16),
            ],
            in_specs=[in_vmem] * 6,
            out_specs=[in_vmem] * 4,
            compiler_params=small,
            name="early_whitening",
        )(raw, first, first_other, second, second_other, band)
        operands = (*operands, third, *last, band)
        kernel, scratch = late_kernel, []
    else:
        operands = (*blocks, band)
        kernel, scratch = cross_kernel, [pltpu.VMEM(shape, jnp.bfloat16) for shape in (padded, spectra)]
    out_shape = (SLOTS, 2, block_rows, block_rows)
    result = pl.pallas_call(
        functools.partial(kernel, spans, 1.0 / math.sqrt(spans * bins2 // 2)),
        out_shape=jax.ShapeDtypeStruct(out_shape, jnp.float32),
        in_specs=[pl.BlockSpec(memory_space=pltpu.SMEM)] + [in_vmem] * len(operands),
        out_specs=in_hbm,
        scratch_shapes=[
            *scratch,
            pltpu.VMEM((2 * block_rows, total[1]), jnp.bfloat16),
            pltpu.VMEM(out_shape, jnp.float32),
            pltpu.SemaphoreType.DMA((SLOTS, 2)),
        ],
        compiler_params=pltpu.CompilerParams(vmem_limit_bytes=24 * 2**20),
        name="cross",
    )(pair_list, *operands)
    return result.reshape(1, SLOTS, 1, 2, block_rows, block_rows)


def solution(mesh):
    placed = (
        P(("days", "chan", "freq"), "tm"),
        P(("days", "chan", "freq"), None),
        P(("chan", "freq"), None),
        P(("days", "chan"), None),
    )

    def step(recording, trailing, whiten_filter, pair_list):
        tables = band_tables(mesh.shape["tm"], mesh.shape["freq"], 2 * trailing.shape[1])
        return jax.shard_map(
            functools.partial(local, tables),
            mesh=mesh,
            in_specs=placed,
            out_specs=P(("days", "chan"), None, ("tm", "freq"), None, None, None),
            check_vma=False,
        )(recording, trailing, whiten_filter, pair_list)

    return step
```

```python
import functools
import math

import jax
import jax.numpy as jnp
import ml_dtypes
import numpy as np
from jax import lax
from jax.experimental import pallas as pl
from jax.experimental.pallas import tpu as pltpu
from jax.sharding import PartitionSpec as P

FB = 512
REACH = 3
SLOTS = 4
LANES = 128


def band_tables(spans, halves, length):
    samples = np.arange(length, dtype=np.int64)[:, None]
    bins = np.arange(FB, dtype=np.int64)[None, :]
    phase = (samples * bins % length).astype(np.float32)
    angle = np.float32(2.0 * math.pi / length) * phase
    ramp = np.float32(2.0 * math.pi / length) * np.arange(length, dtype=np.float32)
    taper = (np.float32(0.5) - np.float32(0.5) * np.cos(ramp))[:, None]
    normaliser = np.float32(1.0 / math.sqrt(0.375 * length))
    cosine = (taper * np.cos(angle) * normaliser).astype(ml_dtypes.bfloat16)
    sine = (-taper * np.sin(angle) * normaliser).astype(ml_dtypes.bfloat16)
    both = np.stack([cosine, sine], axis=1).reshape(length, 2, spans, halves, -1)
    return np.ascontiguousarray(both.transpose(2, 0, 3, 1, 4)).reshape(spans, length, -1)


def swapped(value, axis):
    return lax.ppermute(value, axis, [(0, 1), (1, 0)])


def block_of(own, other):
    low = lax.axis_index("freq") == 0
    a, b = own[...], other[...]
    return jnp.concatenate([jnp.where(low, a, b), jnp.where(low, b, a)], axis=0)


def hop_parts(place, value, table, segments):
    hop = value.shape[1]
    first = jnp.dot(value, table[:hop, :], preferred_element_type=jnp.float32)
    second = jnp.dot(value, table[hop:, :], preferred_element_type=jnp.float32)
    for segment in range(segments):
        yield jnp.where(place == segment, first, jnp.where(place == segment + 1, second, 0.0))


def begin_kernel(recording, trailing, tables, total, table, hop, following, sems):
    span = lax.axis_index("tm")
    width = table.shape[1]
    segments = total.shape[1] // width
    size = hop.shape[1]
    copies = [
        pltpu.make_async_copy(source, target, sems.at[index])
        for index, (source, target) in enumerate(
            (
                (trailing, following),
                (tables.at[span, pl.ds(size, size)], table.at[pl.ds(size, size)]),
                (recording, hop),
                (tables.at[span, pl.ds(0, size)], table.at[pl.ds(0, size)]),
            )
        )
    ]
    for copy in copies:
        copy.start()
    for copy in copies[:2]:
        copy.wait()
    last = jnp.dot(following[...], table[size:, :], preferred_element_type=jnp.float32)
    for copy in copies[2:]:
        copy.wait()
    for segment, value in enumerate(hop_parts(span, hop[...], table, segments)):
        if segment == segments - 1:
            value += last
        total[:, segment * width : (segment + 1) * width] = value


def finish_kernel(spans, *refs):
    hops, (table, begun, mine, theirs, both) = refs[: spans - 1], refs[spans - 1 :]
    rows = mine.shape[0]
    width = table.shape[1]
    part = width // 2
    low = lax.axis_index("freq") == 0
    parts = [
        hop_parts(lax.rem(lax.axis_index("tm") - step + spans, spans), hop[...], table, spans)
        for step, hop in enumerate(hops, 1)
    ]
    for segment, added in enumerate(zip(*parts)):
        value = begun[:, segment * width : (segment + 1) * width]
        for more in added:
            value += more
        first, second = value[:, :part].astype(jnp.bfloat16), value[:, part:].astype(jnp.bfloat16)
        columns = slice(segment * part, (segment + 1) * part)
        mine[:, columns] = both[:rows, columns] = jnp.where(low, first, second)
        theirs[:, columns] = both[rows:, columns] = jnp.where(low, second, first)


def block_kernel(own, other, out):
    out[...] = block_of(own, other)


def lower_kernel(value, out):
    out[...] = value[out.shape[0] :, :]


def band_kernel(chain, *refs):
    *weights, out = refs
    blocks, rows, width = out.shape
    here = lax.axis_index("chan")
    low = lax.axis_index("freq") == 0
    for block in range(blocks):
        if chain == 4:
            own, other = (ref[block].astype(jnp.float32) for ref in weights)
            place = jnp.bitwise_xor(here, (0, 1, 3, 2)[block])
            tile = jnp.concatenate([jnp.where(low, own, other), jnp.where(low, other, own)], axis=1).T
        else:
            place = block
            tile = weights[0][block * rows : (block + 1) * rows, :].astype(jnp.float32)
        blank = jnp.zeros((rows, width - tile.shape[1]), jnp.float32)
        wide = jnp.concatenate([tile, blank], axis=1)
        out[place] = pltpu.roll(wide, 0, 1, stride=1, stride_axis=0).astype(jnp.bfloat16)


def whitened(band, window, raw):
    predicted = jnp.dot(band, window, preferred_element_type=jnp.float32)
    return (raw.astype(jnp.float32) - predicted).astype(jnp.bfloat16)


def pair_products(slots, own, spectra_of, segments, scaling, out, left, result, sems):
    rows, columns = own.shape
    left[:rows, :] = own
    half = columns // (2 * segments)
    turned = []
    for segment in range(segments):
        start = 2 * segment * half
        turned += [own[:, start + half : start + 2 * half], -own[:, start : start + half]]
    left[rows:, :] = jnp.concatenate(turned, axis=1)

    contract = (((1,), (1,)), ((), ()))
    for slot in range(SLOTS):
        partner = slots[0, slot]
        theirs = spectra_of(jnp.maximum(partner, 0))
        for part, lhs in enumerate((left[:rows, :], left[rows:, :])):
            value = lax.dot_general(lhs, theirs, contract, preferred_element_type=jnp.float32)
            result[slot, part] = value * jnp.where(partner >= 0, scaling, 0.0)
            pltpu.make_async_copy(result.at[slot, part], out.at[slot, part], sems.at[slot, part]).start()
    for slot in range(SLOTS):
        for part in range(2):
            pltpu.make_async_copy(result.at[slot, part], out.at[slot, part], sems.at[slot, part]).wait()


def cross_kernel(segments, scaling, slots, *refs):
    near = [0] + [d for d in range(-REACH, REACH + 1) if d]
    blocks, (before, after, band, out, padded, spectra, left, result, sems) = refs[: len(near)], refs[len(near) :]
    count, rows, columns = spectra.shape
    rim = before.shape[0]
    edge = count * rows + rim
    padded[:rim, :] = before[...]
    padded[edge : edge + rim, :] = after[...]
    padded[edge + rim :, :] = jnp.zeros((padded.shape[0] - edge - rim, columns), jnp.bfloat16)
    for distance, value in zip(near, blocks):
        start = (distance + REACH) * rows + rim
        padded[start : start + rows, :] = value[...]
    for block in range(count):
        start = block * rows
        window = padded[start : start + band.shape[2], :]
        spectra[block] = whitened(band[block], window, padded[start + rim : start + rim + rows, :])
    base = lax.axis_index("chan") - REACH
    spectra_of = lambda block: spectra[jnp.clip(block - base, 0, count - 1)]
    pair_products(slots, spectra[REACH], spectra_of, segments, scaling, out, left, result, sems)


def chosen(a, b, c, d):
    here = lax.axis_index("chan")
    return jnp.where(here == 0, a, jnp.where(here == 1, b, jnp.where(here == 2, c, d)))


def early_kernel(raw, first, first_other, second, second_other, band, padded, spectra, beside, middle):
    count, rows, columns = spectra.shape
    rim = (padded.shape[0] - count * rows) // 4
    edge = count * rows + rim
    padded[:rim, :] = jnp.zeros((rim, columns), jnp.bfloat16)
    padded[edge:, :] = jnp.zeros((3 * rim, columns), jnp.bfloat16)
    last = chosen(3, 2, 1, 0)
    padded[pl.ds(pl.multiple_of(last * rows + rim, rim), rows), :] = jnp.zeros((rows, columns), jnp.bfloat16)
    for place, value in (
        (lax.axis_index("chan"), raw),
        (chosen(1, 3, 0, 2), block_of(first, first_other)),
        (chosen(2, 0, 3, 1), block_of(second[: second_other.shape[0], :], second_other)),
    ):
        padded[pl.ds(pl.multiple_of(place * rows + rim, rim), rows), :] = value[...]
    for block in range(count):
        start = block * rows
        window = padded[start : start + band.shape[2], :]
        spectra[block] = whitened(band[block], window, padded[start + rim : start + rim + rows, :])

    window = padded[pl.ds(pl.multiple_of(last * rows, rows), band.shape[2]), :]
    beside[...] = jnp.dot(band[last], window, preferred_element_type=jnp.float32)
    wide = band[last].astype(jnp.float32)
    middle[...] = pltpu.roll(wide, band.shape[2] - rim, 1)[:, :rows].astype(jnp.bfloat16)


def late_kernel(segments, scaling, slots, padded, early, beside, middle, third, fourth, fourth_other, band, out, left, result, sems):
    count, rows, columns = early.shape
    width = band.shape[2]
    rim = (padded.shape[0] - count * rows) // 4
    here = lax.axis_index("chan")
    last = chosen(3, 2, 1, 0)
    inner = (here == 1) | (here == 2)
    value = jnp.where(inner, third[...], block_of(fourth, fourth_other))

    start = pl.multiple_of(last * rows, rows)
    above = padded[pl.ds(start, rim), :]
    below = padded[pl.ds(start + rim + rows, width - rim - rows), :]
    predicted = jnp.dot(middle[...], value, preferred_element_type=jnp.float32) + beside[...]
    arrived = (value.astype(jnp.float32) - predicted).astype(jnp.bfloat16)

    half = rows // 2
    upper = padded[pl.ds(pl.multiple_of(jnp.maximum(start - half, 0), half), half + rim), :]
    window = jnp.concatenate([upper, value[: width - rows - rim]], axis=0)
    bottom = whitened(band[jnp.maximum(last - 1, 0), rows - rim :, half:], window, above)
    lower = below[: LANES - rim]
    window = jnp.concatenate([value[rows - rim :], lower], axis=0)
    top = whitened(band[jnp.minimum(last + 1, count - 1), :rim, :LANES], window, lower[:rim])

    def mended(block, known):
        return jnp.concatenate(
            [
                jnp.where(block == last + 1, top, known[:rim]),
                known[rim : rows - rim],
                jnp.where(block == last - 1, bottom, known[rows - rim :]),
            ],
            axis=0,
        )

    spectra_of = lambda block: mended(block, jnp.where(block == last, arrived, early[block]))
    pair_products(slots, mended(here, early[here]), spectra_of, segments, scaling, out, left, result, sems)


def local(tables, recording, trailing, whiten_filter, pair_list):
    rows, hop = recording.shape
    spans, halves, chain = (lax.axis_size(axis) for axis in ("tm", "freq", "chan"))
    bands = spans * halves
    bins2 = 2 * FB // bands
    block_rows = halves * rows
    taps = whiten_filter.shape[1]
    rim = taps // 2
    here = lax.axis_index("chan")

    in_vmem = pl.BlockSpec(memory_space=pltpu.VMEM)
    small = pltpu.CompilerParams(vmem_limit_bytes=16 * 2**20)

    received = [
        lax.ppermute(recording, "tm", [(i, (i + step) % spans) for i in range(spans)])
        for step in range(1, spans)
    ]
    if chain == 4:
        filters = [
            lax.ppermute(whiten_filter.T, "chan", [(i, i ^ step) for i in range(chain)])
            for step in (1, 3, 2)
        ]
    else:
        filters = [lax.all_gather(whiten_filter, ("chan", "freq"), axis=0, tiled=True)]
    total = (block_rows, spans * bins2)
    in_hbm = pl.BlockSpec(memory_space=pltpu.HBM)
    begun, table = pl.pallas_call(
        begin_kernel,
        out_shape=[
            jax.ShapeDtypeStruct((rows, halves * total[1]), jnp.float32),
            jax.ShapeDtypeStruct(tables.shape[1:], jnp.bfloat16),
        ],
        in_specs=[in_hbm] * 3,
        out_specs=[in_vmem] * 2,
        scratch_shapes=[
            pltpu.VMEM(recording.shape, jnp.bfloat16),
            pltpu.VMEM(trailing.shape, jnp.bfloat16),
            pltpu.SemaphoreType.DMA((4,)),
        ],
        compiler_params=small,
        name="begin_transform",
    )(
        *(
            pltpu.with_memory_space_constraint(value, pltpu.HBM)
            for value in (recording, trailing, jnp.asarray(tables))
        )
    )
    received, filters, begun = lax.optimization_barrier((received, filters, begun))
    half_rows = (rows, total[1])
    mine, theirs, both = pl.pallas_call(
        functools.partial(finish_kernel, spans),
        out_shape=[jax.ShapeDtypeStruct(shape, jnp.bfloat16) for shape in (half_rows, half_rows, total)],
        in_specs=[in_vmem] * (spans + 1),
        out_specs=[in_vmem] * 3,
        compiler_params=small,
        name="finish_transform",
    )(*received, table, begun)
    raw = pl.pallas_call(
        block_kernel,
        out_shape=jax.ShapeDtypeStruct(total, jnp.bfloat16),
        in_specs=[in_vmem] * 2,
        out_specs=in_vmem,
        compiler_params=small,
        name="block",
    )(mine, swapped(theirs, "freq"))

    if chain == 4:
        near = chain
        weights = jnp.stack([whiten_filter.T, *filters])
        weights = (weights, swapped(weights, "freq"))
    else:
        near = 2 * REACH + 1
        beyond = jnp.pad(filters[0], ((REACH * block_rows, REACH * block_rows), (0, 0)))
        weights = (lax.dynamic_slice_in_dim(beyond, here * block_rows, near * block_rows, 0),)
    window = -(-(block_rows + taps) // LANES) * LANES
    band = pl.pallas_call(
        functools.partial(band_kernel, chain),
        out_shape=jax.ShapeDtypeStruct((near, block_rows, window), jnp.bfloat16),
        in_specs=[in_vmem] * len(weights),
        out_specs=in_vmem,
        compiler_params=small,
        name="band_matrix",
    )(*weights)

    if chain == 4:
        route = [(0, 2), (2, 3), (3, 1), (1, 0)]
        first = lax.ppermute(mine, "chan", route)
        across = [(2 * i + half, 2 * j + 1 - half) for i, j in route for half in range(2)]
        first_other = lax.ppermute(theirs, ("chan", "freq"), across)
        second = lax.ppermute(both, "chan", [(1, 3), (3, 2), (2, 0), (0, 1)])
        lower = pl.pallas_call(
            lower_kernel,
            out_shape=jax.ShapeDtypeStruct(half_rows, jnp.bfloat16),
            in_specs=[in_vmem],
            out_specs=in_vmem,
            compiler_params=small,
            name="lower_rows",
        )(second)
        second_other = swapped(lower, "freq")
        third = lax.ppermute(raw, "chan", [(1, 2), (2, 1)])
        last = [lax.ppermute(value, "chan", [(1, 0), (2, 3)]) for value in (first, first_other)]
    else:

        def shifted(value, distance):
            route = [(i - distance, i) for i in range(chain) if 0 <= i - distance < chain]
            return lax.ppermute(value, "chan", route)

        blocks = [raw]
        blocks += [shifted(raw, -d) for d in range(-REACH, REACH + 1) if d]
        blocks.append(shifted(raw[block_rows - rim :, :], REACH + 1))
        blocks.append(shifted(raw[:rim, :], -REACH - 1))

    padded = (near * block_rows + 4 * rim, total[1])
    spectra = (near, *total)
    if chain == 4:
        operands = pl.pallas_call(
            early_kernel,
            out_shape=[
                jax.ShapeDtypeStruct(padded, jnp.bfloat16),
                jax.ShapeDtypeStruct(spectra, jnp.bfloat16),
                jax.ShapeDtypeStruct(total, jnp.float32),
                jax.ShapeDtypeStruct((block_rows, block_rows), jnp.bfloat16),
            ],
            in_specs=[in_vmem] * 6,
            out_specs=[in_vmem] * 4,
            compiler_params=small,
            name="early_whitening",
        )(raw, first, first_other, second, second_other, band)
        operands = (*operands, third, *last, band)
        kernel, scratch = late_kernel, []
    else:
        operands = (*blocks, band)
        kernel, scratch = cross_kernel, [pltpu.VMEM(shape, jnp.bfloat16) for shape in (padded, spectra)]
    out_shape = (SLOTS, 2, block_rows, block_rows)
    result = pl.pallas_call(
        functools.partial(kernel, spans, 1.0 / math.sqrt(spans * bins2 // 2)),
        out_shape=jax.ShapeDtypeStruct(out_shape, jnp.float32),
        in_specs=[pl.BlockSpec(memory_space=pltpu.SMEM)] + [in_vmem] * len(operands),
        out_specs=in_hbm,
        scratch_shapes=[
            *scratch,
            pltpu.VMEM((2 * block_rows, total[1]), jnp.bfloat16),
            pltpu.VMEM(out_shape, jnp.float32),
            pltpu.SemaphoreType.DMA((SLOTS, 2)),
        ],
        compiler_params=pltpu.CompilerParams(vmem_limit_bytes=24 * 2**20),
        name="cross",
    )(pair_list, *operands)
    return result.reshape(1, SLOTS, 1, 2, block_rows, block_rows)


def solution(mesh):
    placed = (
        P(("days", "chan", "freq"), "tm"),
        P(("days", "chan", "freq"), None),
        P(("chan", "freq"), None),
        P(("days", "chan"), None),
    )

    def step(recording, trailing, whiten_filter, pair_list):
        tables = band_tables(mesh.shape["tm"], mesh.shape["freq"], 2 * trailing.shape[1])
        return jax.shard_map(
            functools.partial(local, tables),
            mesh=mesh,
            in_specs=placed,
            out_specs=P(("days", "chan"), None, ("tm", "freq"), None, None, None),
            check_vma=False,
        )(recording, trailing, whiten_filter, pair_list)

    return step
```

```python
import functools
import math

import jax
import jax.numpy as jnp
import ml_dtypes
import numpy as np
from jax import lax
from jax.experimental import pallas as pl
from jax.experimental.pallas import tpu as pltpu
from jax.sharding import PartitionSpec as P

FB = 512
REACH = 3
SLOTS = 4
LANES = 128


def band_tables(spans, halves, length):
    samples = np.arange(length, dtype=np.int64)[:, None]
    bins = np.arange(FB, dtype=np.int64)[None, :]
    phase = (samples * bins % length).astype(np.float32)
    angle = np.float32(2.0 * math.pi / length) * phase
    ramp = np.float32(2.0 * math.pi / length) * np.arange(length, dtype=np.float32)
    taper = (np.float32(0.5) - np.float32(0.5) * np.cos(ramp))[:, None]
    normaliser = np.float32(1.0 / math.sqrt(0.375 * length))
    cosine = (taper * np.cos(angle) * normaliser).astype(ml_dtypes.bfloat16)
    sine = (-taper * np.sin(angle) * normaliser).astype(ml_dtypes.bfloat16)
    both = np.stack([cosine, sine], axis=1).reshape(length, 2, spans, halves, -1)
    return np.ascontiguousarray(both.transpose(2, 0, 3, 1, 4)).reshape(spans, length, -1)


def swapped(value, axis):
    return lax.ppermute(value, axis, [(0, 1), (1, 0)])


def block_of(own, other):
    low = lax.axis_index("freq") == 0
    a, b = own[...], other[...]
    return jnp.concatenate([jnp.where(low, a, b), jnp.where(low, b, a)], axis=0)


def hop_parts(place, value, table, segments):
    hop = value.shape[1]
    first = jnp.dot(value, table[:hop, :], preferred_element_type=jnp.float32)
    second = jnp.dot(value, table[hop:, :], preferred_element_type=jnp.float32)
    for segment in range(segments):
        yield jnp.where(place == segment, first, jnp.where(place == segment + 1, second, 0.0))


def begin_kernel(recording, trailing, tables, total, table, hop, following, sems):
    span = lax.axis_index("tm")
    width = table.shape[1]
    segments = total.shape[1] // width
    size = hop.shape[1]
    copies = [
        pltpu.make_async_copy(source, target, sems.at[index])
        for index, (source, target) in enumerate(
            (
                (trailing, following),
                (tables.at[span, pl.ds(size, size)], table.at[pl.ds(size, size)]),
                (recording, hop),
                (tables.at[span, pl.ds(0, size)], table.at[pl.ds(0, size)]),
            )
        )
    ]
    for copy in copies:
        copy.start()
    for copy in copies[:2]:
        copy.wait()
    last = jnp.dot(following[...], table[size:, :], preferred_element_type=jnp.float32)
    for copy in copies[2:]:
        copy.wait()
    for segment, value in enumerate(hop_parts(span, hop[...], table, segments)):
        if segment == segments - 1:
            value += last
        total[:, segment * width : (segment + 1) * width] = value


def finish_kernel(spans, *refs):
    hops, (table, begun, mine, theirs, both) = refs[: spans - 1], refs[spans - 1 :]
    rows = mine.shape[0]
    width = table.shape[1]
    part = width // 2
    low = lax.axis_index("freq") == 0
    parts = [
        hop_parts(lax.rem(lax.axis_index("tm") - step + spans, spans), hop[...], table, spans)
        for step, hop in enumerate(hops, 1)
    ]
    for segment, added in enumerate(zip(*parts)):
        value = begun[:, segment * width : (segment + 1) * width]
        for more in added:
            value += more
        first, second = value[:, :part].astype(jnp.bfloat16), value[:, part:].astype(jnp.bfloat16)
        columns = slice(segment * part, (segment + 1) * part)
        mine[:, columns] = both[:rows, columns] = jnp.where(low, first, second)
        theirs[:, columns] = both[rows:, columns] = jnp.where(low, second, first)


def block_kernel(own, other, out):
    out[...] = block_of(own, other)


def lower_kernel(value, out):
    out[...] = value[out.shape[0] :, :]


def band_kernel(chain, *refs):
    *weights, out = refs
    blocks, rows, width = out.shape
    here = lax.axis_index("chan")
    low = lax.axis_index("freq") == 0
    for block in range(blocks):
        if chain == 4:
            own, other = (ref[block].astype(jnp.float32) for ref in weights)
            place = jnp.bitwise_xor(here, (0, 1, 3, 2)[block])
            tile = jnp.concatenate([jnp.where(low, own, other), jnp.where(low, other, own)], axis=1).T
        else:
            place = block
            tile = weights[0][block * rows : (block + 1) * rows, :].astype(jnp.float32)
        blank = jnp.zeros((rows, width - tile.shape[1]), jnp.float32)
        wide = jnp.concatenate([tile, blank], axis=1)
        out[place] = pltpu.roll(wide, 0, 1, stride=1, stride_axis=0).astype(jnp.bfloat16)


def whitened(band, window, raw):
    predicted = jnp.dot(band, window, preferred_element_type=jnp.float32)
    return (raw.astype(jnp.float32) - predicted).astype(jnp.bfloat16)


def pair_products(slots, own, spectra_of, segments, scaling, out, left, result, sems):
    rows, columns = own.shape
    left[:rows, :] = own
    half = columns // (2 * segments)
    turned = []
    for segment in range(segments):
        start = 2 * segment * half
        turned += [own[:, start + half : start + 2 * half], -own[:, start : start + half]]
    left[rows:, :] = jnp.concatenate(turned, axis=1)

    contract = (((1,), (1,)), ((), ()))
    for slot in range(SLOTS):
        partner = slots[0, slot]
        theirs = spectra_of(jnp.maximum(partner, 0))
        for part, lhs in enumerate((left[:rows, :], left[rows:, :])):
            value = lax.dot_general(lhs, theirs, contract, preferred_element_type=jnp.float32)
            result[slot, part] = jnp.where(partner >= 0, value * scaling, 0.0)
            pltpu.make_async_copy(result.at[slot, part], out.at[slot, part], sems.at[slot, part]).start()
    for slot in range(SLOTS):
        for part in range(2):
            pltpu.make_async_copy(result.at[slot, part], out.at[slot, part], sems.at[slot, part]).wait()


def cross_kernel(segments, scaling, slots, *refs):
    near = [0] + [d for d in range(-REACH, REACH + 1) if d]
    blocks, (before, after, band, out, padded, spectra, left, result, sems) = refs[: len(near)], refs[len(near) :]
    count, rows, columns = spectra.shape
    rim = before.shape[0]
    edge = count * rows + rim
    padded[:rim, :] = before[...]
    padded[edge : edge + rim, :] = after[...]
    padded[edge + rim :, :] = jnp.zeros((padded.shape[0] - edge - rim, columns), jnp.bfloat16)
    for distance, value in zip(near, blocks):
        start = (distance + REACH) * rows + rim
        padded[start : start + rows, :] = value[...]
    for block in range(count):
        start = block * rows
        window = padded[start : start + band.shape[2], :]
        spectra[block] = whitened(band[block], window, padded[start + rim : start + rim + rows, :])
    base = lax.axis_index("chan") - REACH
    spectra_of = lambda block: spectra[jnp.clip(block - base, 0, count - 1)]
    pair_products(slots, spectra[REACH], spectra_of, segments, scaling, out, left, result, sems)


def chosen(a, b, c, d):
    here = lax.axis_index("chan")
    return jnp.where(here == 0, a, jnp.where(here == 1, b, jnp.where(here == 2, c, d)))


def early_kernel(raw, first, first_other, second, second_other, band, padded, spectra, beside, middle):
    count, rows, columns = spectra.shape
    rim = (padded.shape[0] - count * rows) // 4
    edge = count * rows + rim
    padded[:rim, :] = jnp.zeros((rim, columns), jnp.bfloat16)
    padded[edge:, :] = jnp.zeros((3 * rim, columns), jnp.bfloat16)
    last = chosen(3, 2, 1, 0)
    padded[pl.ds(pl.multiple_of(last * rows + rim, rim), rows), :] = jnp.zeros((rows, columns), jnp.bfloat16)
    for place, value in (
        (lax.axis_index("chan"), raw),
        (chosen(1, 3, 0, 2), block_of(first, first_other)),
        (chosen(2, 0, 3, 1), block_of(second[: second_other.shape[0], :], second_other)),
    ):
        padded[pl.ds(pl.multiple_of(place * rows + rim, rim), rows), :] = value[...]
    for block in range(count):
        start = block * rows
        window = padded[start : start + band.shape[2], :]
        spectra[block] = whitened(band[block], window, padded[start + rim : start + rim + rows, :])

    window = padded[pl.ds(pl.multiple_of(last * rows, rows), band.shape[2]), :]
    beside[...] = jnp.dot(band[last], window, preferred_element_type=jnp.float32)
    wide = band[last].astype(jnp.float32)
    middle[...] = pltpu.roll(wide, band.shape[2] - rim, 1)[:, :rows].astype(jnp.bfloat16)


def late_kernel(segments, scaling, slots, padded, early, beside, middle, third, fourth, fourth_other, band, out, left, result, sems):
    count, rows, columns = early.shape
    width = band.shape[2]
    rim = (padded.shape[0] - count * rows) // 4
    here = lax.axis_index("chan")
    last = chosen(3, 2, 1, 0)
    inner = (here == 1) | (here == 2)
    value = jnp.where(inner, third[...], block_of(fourth, fourth_other))

    start = pl.multiple_of(last * rows, rows)
    above = padded[pl.ds(start, rim), :]
    below = padded[pl.ds(start + rim + rows, width - rim - rows), :]
    predicted = jnp.dot(middle[...], value, preferred_element_type=jnp.float32) + beside[...]
    arrived = (value.astype(jnp.float32) - predicted).astype(jnp.bfloat16)

    half = rows // 2
    upper = padded[pl.ds(pl.multiple_of(jnp.maximum(start - half, 0), half), half + rim), :]
    window = jnp.concatenate([upper, value[: width - rows - rim]], axis=0)
    bottom = whitened(band[jnp.maximum(last - 1, 0), rows - rim :, half:], window, above)
    lower = below[: LANES - rim]
    window = jnp.concatenate([value[rows - rim :], lower], axis=0)
    top = whitened(band[jnp.minimum(last + 1, count - 1), :rim, :LANES], window, lower[:rim])

    def mended(block, known):
        return jnp.concatenate(
            [
                jnp.where(block == last + 1, top, known[:rim]),
                known[rim : rows - rim],
                jnp.where(block == last - 1, bottom, known[rows - rim :]),
            ],
            axis=0,
        )

    spectra_of = lambda block: mended(block, jnp.where(block == last, arrived, early[block]))
    pair_products(slots, mended(here, early[here]), spectra_of, segments, scaling, out, left, result, sems)


def local(tables, recording, trailing, whiten_filter, pair_list):
    rows, hop = recording.shape
    spans, halves, chain = (lax.axis_size(axis) for axis in ("tm", "freq", "chan"))
    bands = spans * halves
    bins2 = 2 * FB // bands
    block_rows = halves * rows
    taps = whiten_filter.shape[1]
    rim = taps // 2
    here = lax.axis_index("chan")

    in_vmem = pl.BlockSpec(memory_space=pltpu.VMEM)
    small = pltpu.CompilerParams(vmem_limit_bytes=16 * 2**20)

    received = [
        lax.ppermute(recording, "tm", [(i, (i + step) % spans) for i in range(spans)])
        for step in range(1, spans)
    ]
    if chain == 4:
        filters = [
            lax.ppermute(whiten_filter.T, "chan", [(i, i ^ step) for i in range(chain)])
            for step in (1, 3, 2)
        ]
    else:
        filters = [lax.all_gather(whiten_filter, ("chan", "freq"), axis=0, tiled=True)]
    total = (block_rows, spans * bins2)
    in_hbm = pl.BlockSpec(memory_space=pltpu.HBM)
    begun, table = pl.pallas_call(
        begin_kernel,
        out_shape=[
            jax.ShapeDtypeStruct((rows, halves * total[1]), jnp.float32),
            jax.ShapeDtypeStruct(tables.shape[1:], jnp.bfloat16),
        ],
        in_specs=[in_hbm] * 3,
        out_specs=[in_vmem] * 2,
        scratch_shapes=[
            pltpu.VMEM(recording.shape, jnp.bfloat16),
            pltpu.VMEM(trailing.shape, jnp.bfloat16),
            pltpu.SemaphoreType.DMA((4,)),
        ],
        compiler_params=small,
        name="begin_transform",
    )(
        *(
            pltpu.with_memory_space_constraint(value, pltpu.HBM)
            for value in (recording, trailing, jnp.asarray(tables))
        )
    )
    received, filters, begun = lax.optimization_barrier((received, filters, begun))
    half_rows = (rows, total[1])
    mine, theirs, both = pl.pallas_call(
        functools.partial(finish_kernel, spans),
        out_shape=[jax.ShapeDtypeStruct(shape, jnp.bfloat16) for shape in (half_rows, half_rows, total)],
        in_specs=[in_vmem] * (spans + 1),
        out_specs=[in_vmem] * 3,
        compiler_params=small,
        name="finish_transform",
    )(*received, table, begun)
    raw = pl.pallas_call(
        block_kernel,
        out_shape=jax.ShapeDtypeStruct(total, jnp.bfloat16),
        in_specs=[in_vmem] * 2,
        out_specs=in_vmem,
        compiler_params=small,
        name="block",
    )(mine, swapped(theirs, "freq"))

    if chain == 4:
        near = chain
        weights = jnp.stack([whiten_filter.T, *filters])
        weights = (weights, swapped(weights, "freq"))
    else:
        near = 2 * REACH + 1
        beyond = jnp.pad(filters[0], ((REACH * block_rows, REACH * block_rows), (0, 0)))
        weights = (lax.dynamic_slice_in_dim(beyond, here * block_rows, near * block_rows, 0),)
    window = -(-(block_rows + taps) // LANES) * LANES
    band = pl.pallas_call(
        functools.partial(band_kernel, chain),
        out_shape=jax.ShapeDtypeStruct((near, block_rows, window), jnp.bfloat16),
        in_specs=[in_vmem] * len(weights),
        out_specs=in_vmem,
        compiler_params=small,
        name="band_matrix",
    )(*weights)

    if chain == 4:
        route = [(0, 2), (2, 3), (3, 1), (1, 0)]
        across = [(2 * i + half, 2 * j + 1 - half) for i, j in route for half in range(2)]
        first_other = lax.ppermute(theirs, ("chan", "freq"), across)
        first = lax.ppermute(mine, "chan", route)
        second = lax.ppermute(both, "chan", [(1, 3), (3, 2), (2, 0), (0, 1)])
        lower = pl.pallas_call(
            lower_kernel,
            out_shape=jax.ShapeDtypeStruct(half_rows, jnp.bfloat16),
            in_specs=[in_vmem],
            out_specs=in_vmem,
            compiler_params=small,
            name="lower_rows",
        )(second)
        second_other = swapped(lower, "freq")
        third = lax.ppermute(raw, "chan", [(1, 2), (2, 1)])
        last = [lax.ppermute(value, "chan", [(1, 0), (2, 3)]) for value in (first, first_other)]
    else:

        def shifted(value, distance):
            route = [(i - distance, i) for i in range(chain) if 0 <= i - distance < chain]
            return lax.ppermute(value, "chan", route)

        blocks = [raw]
        blocks += [shifted(raw, -d) for d in range(-REACH, REACH + 1) if d]
        blocks.append(shifted(raw[block_rows - rim :, :], REACH + 1))
        blocks.append(shifted(raw[:rim, :], -REACH - 1))

    padded = (near * block_rows + 4 * rim, total[1])
    spectra = (near, *total)
    if chain == 4:
        operands = pl.pallas_call(
            early_kernel,
            out_shape=[
                jax.ShapeDtypeStruct(padded, jnp.bfloat16),
                jax.ShapeDtypeStruct(spectra, jnp.bfloat16),
                jax.ShapeDtypeStruct(total, jnp.float32),
                jax.ShapeDtypeStruct((block_rows, block_rows), jnp.bfloat16),
            ],
            in_specs=[in_vmem] * 6,
            out_specs=[in_vmem] * 4,
            compiler_params=small,
            name="early_whitening",
        )(raw, first, first_other, second, second_other, band)
        operands = (*operands, third, *last, band)
        kernel, scratch = late_kernel, []
    else:
        operands = (*blocks, band)
        kernel, scratch = cross_kernel, [pltpu.VMEM(shape, jnp.bfloat16) for shape in (padded, spectra)]
    out_shape = (SLOTS, 2, block_rows, block_rows)
    result = pl.pallas_call(
        functools.partial(kernel, spans, 1.0 / math.sqrt(spans * bins2 // 2)),
        out_shape=jax.ShapeDtypeStruct(out_shape, jnp.float32),
        in_specs=[pl.BlockSpec(memory_space=pltpu.SMEM)] + [in_vmem] * len(operands),
        out_specs=in_hbm,
        scratch_shapes=[
            *scratch,
            pltpu.VMEM((2 * block_rows, total[1]), jnp.bfloat16),
            pltpu.VMEM(out_shape, jnp.float32),
            pltpu.SemaphoreType.DMA((SLOTS, 2)),
        ],
        compiler_params=pltpu.CompilerParams(vmem_limit_bytes=24 * 2**20),
        name="cross",
    )(pair_list, *operands)
    return result.reshape(1, SLOTS, 1, 2, block_rows, block_rows)


def solution(mesh):
    placed = (
        P(("days", "chan", "freq"), "tm"),
        P(("days", "chan", "freq"), None),
        P(("chan", "freq"), None),
        P(("days", "chan"), None),
    )

    def step(recording, trailing, whiten_filter, pair_list):
        tables = band_tables(mesh.shape["tm"], mesh.shape["freq"], 2 * trailing.shape[1])
        return jax.shard_map(
            functools.partial(local, tables),
            mesh=mesh,
            in_specs=placed,
            out_specs=P(("days", "chan"), None, ("tm", "freq"), None, None, None),
            check_vma=False,
        )(recording, trailing, whiten_filter, pair_list)

    return step
```
